32 devices in a mesh: pair: 4 (over y, x), slab: 8 (over z, core).
Axes of the slice: x: 2, y: 2, z: 4, core: 2. Of those that a mesh axis runs over, the one named last changes fastest.
Arguments:
- r_slabs: float32 [12288, 12288], P('slab', 'pair'), may hold values from -2 to 2, as said below
- basis: float32 [12288, 12288], P('slab', 'pair'), may hold values from -0.0546875 to 0.0546875
- owners: int32 [256], P('slab'), may hold values from 0 to 255, as said below
- plan: int32 [2, 64], replicated, may hold values from 0 to 63, as said below
Outputs:
- r_out: float32 [12288, 12288], P('slab', 'pair')
- v_out: float32 [12288, 12288], P('slab', 'pair')
The draws below stay inside these ranges and needn't reach their ends.
Inputs may be any that keep to these rules, and one draw needn't show every extreme that they name: `r_slabs`: in natural row order R is upper triangular with a diagonal between 1 and 2. `owners`: A permutation of the 256 row blocks; of the 32 stored row blocks on each index of slab, exactly 4 belong to the natural range of rows of each index of slab. `plan`: each row is a permutation of the 64 column blocks; slots 2q and 2q + 1 form a pair.
All inputs are finite; a program needn't handle non-finite values.
Results may differ from the reference program's by a relative error of at most 0.0003.
Values sent between devices are 32-bit elements; how exact they have to be, the bound alone decides.
No kernel may reach another device: no remote copies, remote signals or barrier semaphores. Data moves between devices by JAX's collectives and lax.ppermute only.
A program may use at most 192 MiB of HBM per device.

```python
import jax
import jax.numpy as jnp
from jax import lax

N = 12288
BLK = 192
STEPS = 2
ROWB = 48
NBLK = 64
NRB = 256
SLAB_BLOCKS = 32
PAIR_BLOCKS = 16


def owner_table(key):
    slab_count = NRB // SLAB_BLOCKS
    group_size = SLAB_BLOCKS // slab_count
    first_key, second_key = jax.random.split(jax.random.fold_in(key, 7))
    scores = jax.random.permutation(first_key, NRB).reshape(slab_count, SLAB_BLOCKS)
    ranking = jnp.argsort(jnp.argsort(scores, axis=1), axis=1)
    source = (ranking // group_size).reshape(NRB)
    tiebreak = jax.random.permutation(second_key, NRB)
    return jnp.argsort(source * NRB + tiebreak).astype(jnp.int32)


def draw_owners(key, part):
    return owner_table(key)


def draw_r_slabs(key, part):
    table = owner_table(key)
    noise_key, common_key, load_key, diag_key = jax.random.split(jax.random.fold_in(key, 13), 4)
    scale = 1.0 / N ** 0.5
    noise = jax.random.truncated_normal(noise_key, -4.0, 4.0, (N, N), jnp.float32) * scale
    common = jax.random.truncated_normal(common_key, -4.0, 4.0, (N,), jnp.float32) * scale
    loads = jax.random.truncated_normal(load_key, -4.0, 4.0, (N,), jnp.float32) * 1.5
    diagonal = jax.random.uniform(diag_key, (N,), jnp.float32, 1.0, 2.0)
    upper = jnp.triu(noise + common[:, None] * loads[None, :], 1) + jnp.diag(diagonal)
    stored = jnp.take(upper.reshape(NRB, ROWB, N), table, axis=0)
    return stored.reshape(N, N).astype(jnp.float32)


def draw_plan(key, part):
    pair_count = NBLK // PAIR_BLOCKS
    group_size = PAIR_BLOCKS // pair_count
    arrangement = jnp.arange(NBLK, dtype=jnp.int32)
    collected = []
    for step in range(STEPS):
        first_key, second_key = jax.random.split(jax.random.fold_in(key, 100 + step))
        scores = jax.random.permutation(first_key, NBLK).reshape(pair_count, PAIR_BLOCKS)
        ranking = jnp.argsort(jnp.argsort(scores, axis=1), axis=1)
        target = (ranking // group_size).reshape(NBLK)
        order = jnp.argsort(target * NBLK + jax.random.permutation(second_key, NBLK))
        arrangement = jnp.take(arrangement, order)
        collected.append(arrangement)
    return jnp.stack(collected).astype(jnp.int32)


def shard_levels(stream_key, shape, cuts, least, top_value):
    gain = 1.0
    for position, blocks in cuts:
        heights = jax.random.uniform(jax.random.fold_in(jax.random.fold_in(stream_key, 6), position), (blocks,), jnp.float32, least / len(cuts), top_value / len(cuts))
        gain = gain * jnp.repeat(jnp.exp(heights), shape[position] // blocks).reshape((-1,) + (1,) * (len(shape) - 1 - position))
    return gain


def centred(rng, dims, scale, reach, cuts=(), held_as=jnp.bfloat16):
    gain = shard_levels(rng, dims, cuts, -0.22, 0.18) if cuts else 1.0
    values = jax.random.normal(rng, dims, jnp.float32) * scale * gain
    return jnp.minimum(jnp.maximum(values, -reach), reach).astype(held_as)


def setup_inputs(seed: int = 0) -> dict:
    arg_keys = jax.random.split(jax.random.key(seed), 5)
    r_slabs = draw_r_slabs(jax.random.fold_in(arg_keys[4], 71), 0)
    basis = centred(arg_keys[1], (N, N), N ** -0.5, 0.0546875, ((0, 8), (1, 4)), jnp.float32)
    owners = draw_owners(jax.random.fold_in(arg_keys[4], 71), 0)
    plan = draw_plan(jax.random.fold_in(arg_keys[4], 71), 0)
    return dict(r_slabs=r_slabs, basis=basis, owners=owners, plan=plan)


HIGH = lax.Precision.HIGHEST
EPSILON = 1e-06

def rotations(cross_gram, col_norms):
    width = cross_gram.shape[-1]
    scale_a = lax.rsqrt(col_norms[:, :width])
    scale_b = lax.rsqrt(col_norms[:, width:])
    normed = cross_gram * scale_a[:, :, None] * scale_b[:, None, :]
    frobenius = jnp.sqrt(lax.optimization_barrier(jnp.sum(normed * normed, axis=(1, 2))))
    coupling = normed / (1.0 + frobenius)[:, None, None]
    outer_a = jnp.einsum('pik,pjk->pij', coupling, coupling, precision=HIGH)
    outer_b = jnp.einsum('pki,pkj->pij', coupling, coupling, precision=HIGH)
    identity = jnp.eye(width, dtype=cross_gram.dtype)
    left_poly = identity - 0.5 * outer_a + 0.375 * jnp.einsum('pik,pkj->pij', outer_a, outer_a, precision=HIGH)
    right_poly = identity - 0.5 * outer_b + 0.375 * jnp.einsum('pik,pkj->pij', outer_b, outer_b, precision=HIGH)
    upper_half = jnp.concatenate([left_poly, -jnp.einsum('pik,pkj->pij', coupling, right_poly, precision=HIGH)], axis=2)
    lower_half = jnp.concatenate([jnp.einsum('pki,pkj->pij', coupling, left_poly, precision=HIGH), right_poly], axis=2)
    return jnp.concatenate([upper_half, lower_half], axis=1)

def reference(r_slabs, basis, owners, plan):
    stored = r_slabs.reshape(NRB, ROWB, N)
    r_natural = jnp.zeros((NRB, ROWB, N), dtype=r_slabs.dtype).at[owners].set(stored).reshape(N, N)
    a_blocks = r_natural.reshape(N, NBLK, BLK)
    w_blocks = basis.reshape(N, NBLK, BLK)
    for step in range(STEPS):
        order = plan[step]
        a_pairs = jnp.take(a_blocks, order, axis=1).reshape(N, NBLK // 2, 2 * BLK)
        w_pairs = jnp.take(w_blocks, order, axis=1).reshape(N, NBLK // 2, 2 * BLK)
        col_norms = lax.optimization_barrier(jnp.sum(a_pairs * a_pairs, axis=0)) + EPSILON
        cross_gram = jnp.einsum('npi,npj->pij', a_pairs[:, :, :BLK], a_pairs[:, :, BLK:], precision=HIGH)
        turns = rotations(cross_gram, col_norms)
        a_new = jnp.einsum('npk,pkj->npj', a_pairs, turns, precision=HIGH).reshape(N, NBLK, BLK)
        w_new = jnp.einsum('npk,pkj->npj', w_pairs, turns, precision=HIGH).reshape(N, NBLK, BLK)
        if step == STEPS - 1:
            return (a_new.reshape(N, N), w_new.reshape(N, N))
        a_blocks = a_blocks.at[:, order].set(a_new)
        w_blocks = w_blocks.at[:, order].set(w_new)
```

```python
import functools

import jax
import jax.numpy as jnp
from jax import lax
from jax.experimental import pallas as pl
from jax.experimental.pallas import tpu as pltpu
from jax.sharding import PartitionSpec as P

BLK = 192
ROWB = 48
WIN = 256
EPSILON = 1e-06
HIGH = lax.Precision.HIGH
VMEM_LIMIT = 48 * 1024 * 1024


def rotations(cross_gram, norms_a, norms_b):
    width = cross_gram.shape[-1]
    scale_a = lax.rsqrt(norms_a)
    scale_b = lax.rsqrt(norms_b)
    normed = cross_gram * scale_a[:, :, None] * scale_b[:, None, :]
    frobenius = jnp.sqrt(jnp.sum(normed * normed, axis=(1, 2)))
    coupling = normed / (1.0 + frobenius)[:, None, None]
    outer_a = jnp.einsum("pik,pjk->pij", coupling, coupling, precision=HIGH)
    outer_b = jnp.einsum("pki,pkj->pij", coupling, coupling, precision=HIGH)
    identity = jnp.eye(width, dtype=cross_gram.dtype)
    left_poly = (
        identity
        - 0.5 * outer_a
        + 0.375 * jnp.einsum("pik,pkj->pij", outer_a, outer_a, precision=HIGH)
    )
    right_poly = (
        identity
        - 0.5 * outer_b
        + 0.375 * jnp.einsum("pik,pkj->pij", outer_b, outer_b, precision=HIGH)
    )
    upper_half = jnp.concatenate(
        [left_poly, -jnp.einsum("pik,pkj->pij", coupling, right_poly, precision=HIGH)], axis=2
    )
    lower_half = jnp.concatenate(
        [jnp.einsum("pki,pkj->pij", coupling, left_poly, precision=HIGH), right_poly], axis=2
    )
    return jnp.concatenate([upper_half, lower_half], axis=1)


def turns_of(sums):
    cross_gram = sums[:, :BLK, :BLK]
    norms_a = sums[:, BLK, :BLK] + EPSILON
    norms_b = sums[:, BLK + 1, :BLK] + EPSILON
    return rotations(cross_gram, norms_a, norms_b)


def move_tables(place, me, groups, count):
    total = place.shape[0]
    units = count // groups
    slots = jnp.arange(total, dtype=jnp.int32)
    source, local = place // count, place % count
    target = slots // count
    same = (target[:, None] == target[None, :]) & (source[:, None] == source[None, :])
    rank = jnp.sum((same & (slots[None, :] < slots[:, None])).astype(jnp.int32), axis=1)
    offset = jnp.arange(groups, dtype=jnp.int32)
    unit = jnp.arange(units, dtype=jnp.int32)
    chosen = (
        (source == me)[None, None, :]
        & (target[None, None, :] == (me ^ offset)[:, None, None])
        & (rank[None, None, :] == unit[None, :, None])
    )
    send = jnp.sum(jnp.where(chosen, local[None, None, :], 0), axis=2).reshape(groups * units)
    mine = lax.dynamic_slice_in_dim(source ^ me, me * count, count)
    order = lax.dynamic_slice_in_dim(rank, me * count, count)
    return send, mine, order


def rank_among(kind):
    index = jnp.arange(kind.shape[-1], dtype=jnp.int32)
    same = (kind[..., :, None] == kind[..., None, :]) & (index[None, :] < index[:, None])
    return jnp.sum(same.astype(jnp.int32), axis=-1)


def shifted(window, left):
    return pltpu.roll(window, WIN - 64 if left else 64, 1)


def low_half(window, odd):
    return jnp.where(odd == 1, shifted(window, True), window)


def merge(first, first_odd, second, second_odd):
    a = low_half(first, first_odd)
    b = jnp.where(second_odd == 1, second, shifted(second, False))
    lane = lax.broadcasted_iota(jnp.int32, (first.shape[0], 128), 1)
    middle = jnp.where(lane < 64, a[:, 128:], b[:, :128])
    return jnp.concatenate([a[:, :128], middle, b[:, 128:]], axis=1)


def unit_width(units):
    return max(WIN, units * BLK)


def pack_kernel(groups, units, blocks, send, rows_at, *refs):
    sources, outs = refs[:blocks], refs[blocks:]
    size = sources[0].shape[0]
    for i, x_ref in enumerate(sources):
        rows = slice(i * size, (i + 1) * size)

        def window(place):
            block = send[place]
            strip = (3 * block) // 2
            return x_ref[:, pl.ds(pl.multiple_of(strip * 128, 128), WIN)], block % 2

        for group in range(groups):
            if units == 1:
                w, odd = window(group)
                outs[group][rows, :] = low_half(w, odd)
            for j in range(0, units - 1, 2):
                w0, odd0 = window(group * units + j)
                w1, odd1 = window(group * units + j + 1)
                outs[group][rows, BLK * j : BLK * (j + 2)] = merge(w0, odd0, w1, odd1)


def pack(x, send, rows_at, block_rows, groups, units):
    total = rows_at.shape[0]
    blocks = 4 if total % 4 == 0 else 1
    width = unit_width(units)

    def block_at(k):
        return pl.BlockSpec(
            (block_rows, x.shape[1]), lambda i, send, at: (at[i * blocks + k], 0)
        )

    return pl.pallas_call(
        functools.partial(pack_kernel, groups, units, blocks),
        grid_spec=pltpu.PrefetchScalarGridSpec(
            num_scalar_prefetch=2,
            grid=(total // blocks,),
            in_specs=[block_at(k) for k in range(blocks)],
            out_specs=[pl.BlockSpec((blocks * block_rows, width), lambda i, *_: (i, 0))]
            * groups,
        ),
        out_shape=[jax.ShapeDtypeStruct((total * block_rows, width), jnp.float32)] * groups,
        compiler_params=pltpu.CompilerParams(vmem_limit_bytes=VMEM_LIMIT),
        cost_estimate=pl.CostEstimate(
            flops=0,
            bytes_accessed=2 * 4 * total * block_rows * x.shape[1],
            transcendentals=0,
        ),
        name="pack",
    )(send, rows_at, *[x] * blocks)


def halves(x):
    high = x.astype(jnp.bfloat16)
    return high, (x - high.astype(jnp.float32)).astype(jnp.bfloat16)


def product(a, b, dims):
    (ah, al), (bh, bl) = a, b
    dot = functools.partial(
        lax.dot_general, dimension_numbers=(dims, ((), ())), preferred_element_type=jnp.float32
    )
    return dot(ah, bh) + (dot(al, bh) + dot(ah, bl))


def fetcher(arrive, order, sources, win, sems, row0, rows):
    def start(q, slot):
        for side in range(2):
            at = arrive[2 * q + side]
            strip = (3 * order[2 * q + side]) // 2
            for k, source in enumerate(sources):

                @pl.when(at == k)
                def _():
                    pltpu.make_async_copy(
                        source.at[
                            pl.ds(row0, rows), pl.ds(pl.multiple_of(strip * 128, 128), WIN)
                        ],
                        win.at[slot, side],
                        sems.at[slot, side],
                    ).start()

    def wait(slot):
        for side in range(2):
            pltpu.make_async_copy(
                sources[0].at[pl.ds(row0, rows), pl.ds(0, WIN)],
                win.at[slot, side],
                sems.at[slot, side],
            ).wait()

    return start, wait


def pipelined(start, wait):
    q, last = pl.program_id(0), pl.num_programs(0)
    slot = lax.rem(q, 2)

    @pl.when(q == 0)
    def _():
        start(0, 0)

    @pl.when(q + 1 < last)
    def _():
        start(q + 1, 1 - slot)

    wait(slot)
    return q, slot


def tile_of(rows):
    return 256 if rows % 256 == 0 else rows


def pair_tile(win, slot, start, tile):
    rows = pl.ds(pl.multiple_of(start, 8), tile)
    return jnp.concatenate([win[slot, 0, rows, :], win[slot, 1, rows, :]], axis=1)


def spread(turn, odd, other_odd):
    gap = jnp.zeros((WIN - BLK, 2 * BLK), jnp.float32)

    def placed(part, odd):
        return jnp.where(
            odd == 1, jnp.concatenate([gap, part]), jnp.concatenate([part, gap])
        )

    return jnp.concatenate([placed(turn[:BLK], odd), placed(turn[BLK:], other_odd)])


def long_halves(turn):
    high, low = halves(turn)
    return jnp.concatenate([high, high, low])


def turned_tile(x, long_turn):
    high, low = halves(x)
    return jnp.dot(
        jnp.concatenate([high, low, high], axis=1), long_turn, preferred_element_type=jnp.float32
    )


def gram_kernel(groups, arrive, order, *refs):
    sources, (out, win, sems) = refs[:groups], refs[groups:]
    rows = win.shape[2]
    q, slot = pipelined(*fetcher(arrive, order, sources, win, sems, 0, rows))
    tile = tile_of(rows)
    total = jnp.zeros((WIN, WIN), jnp.float32)
    squares = jnp.zeros((8, 2 * WIN), jnp.float32)
    for step in range(rows // tile):
        x = pair_tile(win, slot, step * tile, tile)
        high, low = halves(x)
        total += product(
            (high[:, :WIN], low[:, :WIN]), (high[:, WIN:], low[:, WIN:]), ((0,), (0,))
        )
        squares += jnp.sum((x * x).reshape(tile // 8, 8, 2 * WIN), axis=0)
    odd, other_odd = order[2 * q] % 2, order[2 * q + 1] % 2
    total = jnp.where(odd == 1, total[WIN - BLK :], total[:BLK])
    out[0, :BLK, :] = low_half(total, other_odd)
    norms = jnp.broadcast_to(jnp.sum(squares, axis=0, keepdims=True), (8, 2 * WIN))
    row = lax.broadcasted_iota(jnp.int32, (8, WIN), 0)
    out[0, BLK:, :] = jnp.where(
        row == 0, low_half(norms[:, :WIN], odd), low_half(norms[:, WIN:], other_odd)
    )


def gram(sources, arrive, order):
    groups, rows = len(sources), sources[0].shape[0]
    pairs = arrive.shape[0] // 2
    return pl.pallas_call(
        functools.partial(gram_kernel, groups),
        grid_spec=pltpu.PrefetchScalarGridSpec(
            num_scalar_prefetch=2,
            grid=(pairs,),
            in_specs=[pl.BlockSpec(memory_space=pl.ANY)] * groups,
            out_specs=pl.BlockSpec((1, BLK + 8, WIN), lambda q, *_: (q, 0, 0)),
            scratch_shapes=[
                pltpu.VMEM((2, 2, rows, WIN), jnp.float32),
                pltpu.SemaphoreType.DMA((2, 2)),
            ],
        ),
        out_shape=jax.ShapeDtypeStruct((pairs, BLK + 8, WIN), jnp.float32),
        compiler_params=pltpu.CompilerParams(vmem_limit_bytes=VMEM_LIMIT),
        cost_estimate=pl.CostEstimate(
            flops=6 * pairs * rows * WIN * WIN,
            bytes_accessed=8 * pairs * rows * WIN,
            transcendentals=0,
        ),
        name="cross_products",
    )(arrive, order, *sources)


def rotate_kernel(groups, row0, given, arrive, order, *refs):
    sources, turn = refs[:groups], refs[groups]
    out, win, sems = refs[groups + 1 + given :]
    rows = win.shape[2]
    q, slot = pipelined(*fetcher(arrive, order, sources, win, sems, row0, rows))
    tile = tile_of(rows)
    long_turn = long_halves(spread(turn[0], order[2 * q] % 2, order[2 * q + 1] % 2))
    for step in range(rows // tile):
        x = pair_tile(win, slot, step * tile, tile)
        out[step * tile : (step + 1) * tile, :] = turned_tile(x, long_turn)


def rotate(sources, arrive, order, turns, row0, rows, into=None, shape=None, at=0):
    groups = len(sources)
    pairs = arrive.shape[0] // 2
    shape = shape or (rows, pairs * 2 * BLK)
    given = [] if into is None else [into]
    return pl.pallas_call(
        functools.partial(rotate_kernel, groups, row0, len(given)),
        grid_spec=pltpu.PrefetchScalarGridSpec(
            num_scalar_prefetch=2,
            grid=(pairs,),
            in_specs=[pl.BlockSpec(memory_space=pl.ANY)] * groups
            + [pl.BlockSpec((1, 2 * BLK, 2 * BLK), lambda q, *_: (q, 0, 0))]
            + [pl.BlockSpec(memory_space=pl.ANY)] * len(given),
            out_specs=pl.BlockSpec((rows, 2 * BLK), lambda q, *_: (at, q)),
            scratch_shapes=[
                pltpu.VMEM((2, 2, rows, WIN), jnp.float32),
                pltpu.SemaphoreType.DMA((2, 2)),
            ],
        ),
        out_shape=jax.ShapeDtypeStruct(shape, jnp.float32),
        input_output_aliases={groups + 3: 0} if given else {},
        compiler_params=pltpu.CompilerParams(vmem_limit_bytes=VMEM_LIMIT),
        cost_estimate=pl.CostEstimate(
            flops=6 * pairs * rows * 4 * BLK * BLK,
            bytes_accessed=4 * pairs * rows * (2 * WIN + 2 * BLK),
            transcendentals=0,
        ),
        name="rotate",
    )(arrive, order, *sources, turns, *given)


def slab_pack_kernel(groups, *refs):
    sources, (out, held, in_sems, out_sems) = refs[:groups], refs[groups:]
    slabs, rows, _ = out.shape
    width = sources[0].shape[1]
    arrivals = []
    for o in range(slabs):
        for g in range(groups):
            copy = pltpu.make_async_copy(
                sources[g].at[pl.ds(o * rows, rows), :],
                held.at[o, :, pl.ds(g * width, width)],
                in_sems.at[o, g],
            )
            copy.start()
            arrivals.append(copy)
    departures = []
    for o in range(slabs):
        for copy in arrivals[o * groups : (o + 1) * groups]:
            copy.wait()
        copy = pltpu.make_async_copy(held.at[o], out.at[o], out_sems.at[o])
        copy.start()
        departures.append(copy)
    for copy in departures:
        copy.wait()


def slab_pack(sources, slabs):
    groups = len(sources)
    rows, width = sources[0].shape[0] // slabs, sources[0].shape[1]
    shape = (slabs, rows, groups * width)
    return pl.pallas_call(
        functools.partial(slab_pack_kernel, groups),
        in_specs=[pl.BlockSpec(memory_space=pl.ANY)] * groups,
        out_specs=pl.BlockSpec(memory_space=pl.ANY),
        scratch_shapes=[
            pltpu.VMEM(shape, jnp.float32),
            pltpu.SemaphoreType.DMA((slabs, groups)),
            pltpu.SemaphoreType.DMA((slabs,)),
        ],
        out_shape=jax.ShapeDtypeStruct(shape, jnp.float32),
        compiler_params=pltpu.CompilerParams(vmem_limit_bytes=VMEM_LIMIT),
        cost_estimate=pl.CostEstimate(
            flops=0, bytes_accessed=8 * slabs * rows * groups * width, transcendentals=0
        ),
        name="slab_pack",
    )(*sources)


def settle_kernel(strips, given, arrive, order, natural, source, turn, *refs):
    out, win, done, sems, out_sems = refs[given:]
    rows = source.shape[0]

    def start(q, slot):
        for side in range(2):
            strip = arrive[2 * q + side] * strips + (3 * order[2 * q + side]) // 2
            columns = pl.ds(pl.multiple_of(strip * 128, 128), WIN)
            pltpu.make_async_copy(
                source.at[:, columns], win.at[slot, side], sems.at[slot, side]
            ).start()

    def wait(slot):
        for side in range(2):
            pltpu.make_async_copy(
                source.at[:, pl.ds(0, WIN)], win.at[slot, side], sems.at[slot, side]
            ).wait()

    q, slot = pipelined(start, wait)
    tile = tile_of(rows)
    long_turn = long_halves(spread(turn[0], order[2 * q] % 2, order[2 * q + 1] % 2))

    def written(at):
        pltpu.make_async_copy(done.at[at], done.at[at], out_sems.at[at]).wait()

    @pl.when(q >= 2)
    def _():
        written(slot)

    for step in range(rows // tile):
        x = pair_tile(win, slot, step * tile, tile)
        done[slot, step * tile : (step + 1) * tile, :] = turned_tile(x, long_turn)

    columns = pl.ds(pl.multiple_of(q * 2 * BLK, 128), 2 * BLK)
    for block in range(rows // ROWB):
        pltpu.make_async_copy(
            done.at[slot, pl.ds(block * ROWB, ROWB), :],
            out.at[pl.ds(pl.multiple_of(natural[block] * ROWB, 8), ROWB), columns],
            out_sems.at[slot],
        ).start()

    @pl.when(q == pl.num_programs(0) - 1)
    def _():
        written(slot)

        @pl.when(q >= 1)
        def _():
            written(1 - slot)


def settle(source, arrive, order, natural, turns, strips, shape, into=None):
    source = source.reshape(-1, source.shape[2])
    rows = source.shape[0]
    pairs = arrive.shape[0] // 2
    given = [] if into is None else [into]
    return pl.pallas_call(
        functools.partial(settle_kernel, strips, len(given)),
        grid_spec=pltpu.PrefetchScalarGridSpec(
            num_scalar_prefetch=3,
            grid=(pairs,),
            in_specs=[pl.BlockSpec(memory_space=pl.ANY)]
            + [pl.BlockSpec((1, 2 * BLK, 2 * BLK), lambda q, *_: (q, 0, 0))]
            + [pl.BlockSpec(memory_space=pl.ANY)] * len(given),
            out_specs=pl.BlockSpec(memory_space=pl.ANY),
            scratch_shapes=[
                pltpu.VMEM((2, 2, rows, WIN), jnp.float32),
                pltpu.VMEM((2, rows, 2 * BLK), jnp.float32),
                pltpu.SemaphoreType.DMA((2, 2)),
                pltpu.SemaphoreType.DMA((2,)),
            ],
        ),
        out_shape=jax.ShapeDtypeStruct(shape, jnp.float32),
        input_output_aliases={5: 0} if given else {},
        compiler_params=pltpu.CompilerParams(vmem_limit_bytes=VMEM_LIMIT),
        cost_estimate=pl.CostEstimate(
            flops=6 * pairs * rows * 4 * BLK * BLK,
            bytes_accessed=4 * pairs * rows * (2 * WIN + 2 * BLK),
            transcendentals=0,
        ),
        name="settle",
    )(arrive, order, natural, source, turns, *given)


def swap(arrays, axis):
    count = len(arrays)
    return [arrays[0]] + [
        lax.ppermute(arrays[o], axis, [(i, i ^ o) for i in range(count)]) for o in range(1, count)
    ]


def after(arrays, earlier):
    arrays, earlier = lax.optimization_barrier((list(arrays), list(earlier)))
    return arrays, earlier


def shards(groups, slabs, r_slabs, basis, owners, plan):
    rows = r_slabs.shape[0]
    count = r_slabs.shape[1] // BLK
    units = count // groups
    strips = unit_width(units) // 128
    row_blocks = owners.shape[0]
    each = row_blocks // slabs
    chunks = 2 if each % 2 == 0 else 1
    per = each // chunks
    part = rows // chunks
    pair_index = lax.axis_index("pair")
    slab_index = lax.axis_index("slab")

    send_0, arrive_0, order_0 = move_tables(plan[0], pair_index, groups, count)
    slot_ids = jnp.arange(plan.shape[1], dtype=jnp.int32)
    place_1 = jnp.sum(
        jnp.where(plan[0][None, :] == plan[1][:, None], slot_ids[None, :], 0), axis=1
    )
    send_1, arrive_1, order_1 = move_tables(place_1, pair_index, groups, count)

    goes_to = owners // row_blocks
    rank = rank_among(goes_to)
    spot = (rank // per) * (slabs * per) + goes_to * per + rank % per
    index = jnp.arange(row_blocks, dtype=jnp.int32)
    rows_at = jnp.sum(jnp.where(spot[None, :] == index[:, None], index[None, :], 0), axis=1)
    table = lax.all_gather(owners, "slab", axis=0, tiled=True).reshape(slabs, row_blocks)
    table_to = table // row_blocks
    table_rank = rank_among(table_to)
    per_rank = jnp.arange(each, dtype=jnp.int32)
    hit = (table_to == slab_index)[:, None, :] & (table_rank[:, None, :] == per_rank[None, :, None])
    where_to = jnp.sum(jnp.where(hit, (table % row_blocks)[:, None, :], 0), axis=2)
    natural = [
        where_to[:, c * per : (c + 1) * per].reshape(slabs * per) for c in range(chunks)
    ]

    steps = part // ROWB
    straight = [
        jnp.arange(steps, dtype=jnp.int32) + c * steps for c in range(chunks)
    ]

    def summed(*parts):
        return lax.psum(functools.reduce(jnp.add, parts), "slab")

    r_sent = pack(r_slabs, send_0, rows_at, ROWB, groups, units)
    r_got = swap(r_sent, "pair")
    v_sent = [pack(basis, send_0, straight[c], ROWB, groups, units) for c in range(chunks)]

    v_got = [None] * chunks
    v_sent[0], (r_got, natural) = after(v_sent[0], (r_got, natural))
    v_got[0] = swap(v_sent[0], "pair")
    turns = turns_of(summed(gram(r_got, arrive_0, order_0)))

    def second(sources, row0):
        turned = rotate(sources, arrive_0, order_0, turns, row0, part)
        return pack(turned, send_1, straight[0], ROWB, groups, units)

    r_two = []
    for c in range(chunks):
        sent = second(r_got, c * part)
        if c == 0:
            sent, v_got[0] = after(sent, v_got[0])
        else:
            sent, r_two[-1] = after(sent, r_two[-1])
        r_two.append(swap(sent, "pair"))
    for c in range(1, chunks):
        v_sent[c], r_two[-1] = after(v_sent[c], r_two[-1])
        v_got[c] = swap(v_sent[c], "pair")

    v_next = [second(v_got[0], 0)]
    packed = [slab_pack(r_two[c], slabs) for c in range(chunks)]
    sums = functools.reduce(jnp.add, [gram(r_two[c], arrive_1, order_1) for c in range(chunks)])
    (v_next[0], packed[1:], sums), v_got[-1] = after((v_next[0], packed[1:], sums), v_got[-1])
    r_home = [lax.all_to_all(packed[c], "slab", 0, 0, tiled=True) for c in range(chunks)]
    v_two = [swap(v_next[0], "pair")]
    turns_1 = turns_of(summed(sums))
    for c in range(1, chunks):
        sent, v_two[-1] = after(second(v_got[c], 0), v_two[-1])
        v_two.append(swap(sent, "pair"))

    r_out = v_out = None
    for c in range(chunks):
        if c > 0:
            (v_two[c], r_home[c]), (r_out, v_out) = after((v_two[c], r_home[c]), (r_out, v_out))
        r_out = settle(
            r_home[c], arrive_1, order_1, natural[c], turns_1, strips, r_slabs.shape, r_out
        )
        v_out = rotate(v_two[c], arrive_1, order_1, turns_1, 0, part, v_out, basis.shape, c)
    return r_out, v_out


def solution(mesh):
    placed = (P("slab", "pair"), P("slab", "pair"), P("slab"), P())
    return jax.shard_map(
        functools.partial(shards, mesh.shape["pair"], mesh.shape["slab"]),
        mesh=mesh,
        in_specs=placed,
        out_specs=(P("slab", "pair"), P("slab", "pair")),
        check_vma=False,
    )
```

```python
import functools

import jax
import jax.numpy as jnp
from jax import lax
from jax.experimental import pallas as pl
from jax.experimental.pallas import tpu as pltpu
from jax.sharding import PartitionSpec as P

BLK = 192
ROWB = 48
WIN = 256
EPSILON = 1e-06
HIGH = lax.Precision.HIGH
VMEM_LIMIT = 48 * 1024 * 1024


def rotations(cross_gram, norms_a, norms_b):
    width = cross_gram.shape[-1]
    scale_a = lax.rsqrt(norms_a)
    scale_b = lax.rsqrt(norms_b)
    normed = cross_gram * scale_a[:, :, None] * scale_b[:, None, :]
    frobenius = jnp.sqrt(jnp.sum(normed * normed, axis=(1, 2)))
    coupling = normed / (1.0 + frobenius)[:, None, None]
    outer_a = jnp.einsum("pik,pjk->pij", coupling, coupling, precision=HIGH)
    outer_b = jnp.einsum("pki,pkj->pij", coupling, coupling, precision=HIGH)
    identity = jnp.eye(width, dtype=cross_gram.dtype)
    left_poly = (
        identity
        - 0.5 * outer_a
        + 0.375 * jnp.einsum("pik,pkj->pij", outer_a, outer_a, precision=HIGH)
    )
    right_poly = (
        identity
        - 0.5 * outer_b
        + 0.375 * jnp.einsum("pik,pkj->pij", outer_b, outer_b, precision=HIGH)
    )
    upper_half = jnp.concatenate(
        [left_poly, -jnp.einsum("pik,pkj->pij", coupling, right_poly, precision=HIGH)], axis=2
    )
    lower_half = jnp.concatenate(
        [jnp.einsum("pki,pkj->pij", coupling, left_poly, precision=HIGH), right_poly], axis=2
    )
    return jnp.concatenate([upper_half, lower_half], axis=1)


def turns_of(sums):
    cross_gram = sums[:, :BLK, :BLK]
    norms_a = sums[:, BLK, :BLK] + EPSILON
    norms_b = sums[:, BLK + 1, :BLK] + EPSILON
    return rotations(cross_gram, norms_a, norms_b)


def move_tables(place, me, groups, count):
    total = place.shape[0]
    units = count // groups
    slots = jnp.arange(total, dtype=jnp.int32)
    source, local = place // count, place % count
    target = slots // count
    same = (target[:, None] == target[None, :]) & (source[:, None] == source[None, :])
    rank = jnp.sum((same & (slots[None, :] < slots[:, None])).astype(jnp.int32), axis=1)
    offset = jnp.arange(groups, dtype=jnp.int32)
    unit = jnp.arange(units, dtype=jnp.int32)
    chosen = (
        (source == me)[None, None, :]
        & (target[None, None, :] == (me ^ offset)[:, None, None])
        & (rank[None, None, :] == unit[None, :, None])
    )
    send = jnp.sum(jnp.where(chosen, local[None, None, :], 0), axis=2).reshape(groups * units)
    mine = lax.dynamic_slice_in_dim(source ^ me, me * count, count)
    order = lax.dynamic_slice_in_dim(rank, me * count, count)
    return send, mine, order


def rank_among(kind):
    index = jnp.arange(kind.shape[-1], dtype=jnp.int32)
    same = (kind[..., :, None] == kind[..., None, :]) & (index[None, :] < index[:, None])
    return jnp.sum(same.astype(jnp.int32), axis=-1)


def shifted(window, left):
    return pltpu.roll(window, WIN - 64 if left else 64, 1)


def low_half(window, odd):
    return jnp.where(odd == 1, shifted(window, True), window)


def merge(first, first_odd, second, second_odd):
    a = low_half(first, first_odd)
    b = jnp.where(second_odd == 1, second, shifted(second, False))
    lane = lax.broadcasted_iota(jnp.int32, (first.shape[0], 128), 1)
    middle = jnp.where(lane < 64, a[:, 128:], b[:, :128])
    return jnp.concatenate([a[:, :128], middle, b[:, 128:]], axis=1)


def unit_width(units):
    return max(WIN, units * BLK)


def pack_kernel(groups, units, blocks, send, rows_at, *refs):
    sources, outs = refs[:blocks], refs[blocks:]
    size = sources[0].shape[0]
    for i, x_ref in enumerate(sources):
        rows = slice(i * size, (i + 1) * size)

        def window(place):
            block = send[place]
            strip = (3 * block) // 2
            return x_ref[:, pl.ds(pl.multiple_of(strip * 128, 128), WIN)], block % 2

        for group in range(groups):
            if units == 1:
                w, odd = window(group)
                outs[group][rows, :] = low_half(w, odd)
            for j in range(0, units - 1, 2):
                w0, odd0 = window(group * units + j)
                w1, odd1 = window(group * units + j + 1)
                outs[group][rows, BLK * j : BLK * (j + 2)] = merge(w0, odd0, w1, odd1)


def pack(x, send, rows_at, block_rows, groups, units):
    total = rows_at.shape[0]
    blocks = 4 if total % 4 == 0 else 1
    width = unit_width(units)

    def block_at(k):
        return pl.BlockSpec(
            (block_rows, x.shape[1]), lambda i, send, at: (at[i * blocks + k], 0)
        )

    return pl.pallas_call(
        functools.partial(pack_kernel, groups, units, blocks),
        grid_spec=pltpu.PrefetchScalarGridSpec(
            num_scalar_prefetch=2,
            grid=(total // blocks,),
            in_specs=[block_at(k) for k in range(blocks)],
            out_specs=[pl.BlockSpec((blocks * block_rows, width), lambda i, *_: (i, 0))]
            * groups,
        ),
        out_shape=[jax.ShapeDtypeStruct((total * block_rows, width), jnp.float32)] * groups,
        compiler_params=pltpu.CompilerParams(vmem_limit_bytes=VMEM_LIMIT),
        cost_estimate=pl.CostEstimate(
            flops=0,
            bytes_accessed=2 * 4 * total * block_rows * x.shape[1],
            transcendentals=0,
        ),
        name="pack",
    )(send, rows_at, *[x] * blocks)


def halves(x):
    high = x.astype(jnp.bfloat16)
    return high, (x - high.astype(jnp.float32)).astype(jnp.bfloat16)


def product(a, b, dims):
    (ah, al), (bh, bl) = a, b
    dot = functools.partial(
        lax.dot_general, dimension_numbers=(dims, ((), ())), preferred_element_type=jnp.float32
    )
    return dot(ah, bh) + (dot(al, bh) + dot(ah, bl))


def fetcher(arrive, order, sources, win, sems, row0, rows):
    def start(q, slot):
        for side in range(2):
            at = arrive[2 * q + side]
            strip = (3 * order[2 * q + side]) // 2
            for k, source in enumerate(sources):

                @pl.when(at == k)
                def _():
                    pltpu.make_async_copy(
                        source.at[
                            pl.ds(row0, rows), pl.ds(pl.multiple_of(strip * 128, 128), WIN)
                        ],
                        win.at[slot, side],
                        sems.at[slot, side],
                    ).start()

    def wait(slot):
        for side in range(2):
            pltpu.make_async_copy(
                sources[0].at[pl.ds(row0, rows), pl.ds(0, WIN)],
                win.at[slot, side],
                sems.at[slot, side],
            ).wait()

    return start, wait


def pipelined(start, wait):
    q, last = pl.program_id(0), pl.num_programs(0)
    slot = lax.rem(q, 2)

    @pl.when(q == 0)
    def _():
        start(0, 0)

    @pl.when(q + 1 < last)
    def _():
        start(q + 1, 1 - slot)

    wait(slot)
    return q, slot


def tile_of(rows):
    return 384 if rows % 384 == 0 else rows


def pair_tile(win, slot, start, tile):
    rows = pl.ds(pl.multiple_of(start, 8), tile)
    return jnp.concatenate([win[slot, 0, rows, :], win[slot, 1, rows, :]], axis=1)


def spread(turn, odd, other_odd):
    gap = jnp.zeros((WIN - BLK, 2 * BLK), jnp.float32)

    def placed(part, odd):
        return jnp.where(
            odd == 1, jnp.concatenate([gap, part]), jnp.concatenate([part, gap])
        )

    return jnp.concatenate([placed(turn[:BLK], odd), placed(turn[BLK:], other_odd)])


def long_halves(turn):
    high, low = halves(turn)
    return jnp.concatenate([high, high, low])


def turned_tile(x, long_turn):
    high, low = halves(x)
    return jnp.dot(
        jnp.concatenate([high, low, high], axis=1), long_turn, preferred_element_type=jnp.float32
    )


def gram_kernel(groups, arrive, order, *refs):
    sources, (out, win, sems) = refs[:groups], refs[groups:]
    rows = win.shape[2]
    q, slot = pipelined(*fetcher(arrive, order, sources, win, sems, 0, rows))
    tile = tile_of(rows)
    total = jnp.zeros((WIN, WIN), jnp.float32)
    squares = jnp.zeros((8, 2 * WIN), jnp.float32)
    for step in range(rows // tile):
        x = pair_tile(win, slot, step * tile, tile)
        high, low = halves(x)
        total += product(
            (high[:, :WIN], low[:, :WIN]), (high[:, WIN:], low[:, WIN:]), ((0,), (0,))
        )
        squares += jnp.sum((x * x).reshape(tile // 8, 8, 2 * WIN), axis=0)
    odd, other_odd = order[2 * q] % 2, order[2 * q + 1] % 2
    total = jnp.where(odd == 1, total[WIN - BLK :], total[:BLK])
    out[0, :BLK, :] = low_half(total, other_odd)
    norms = jnp.broadcast_to(jnp.sum(squares, axis=0, keepdims=True), (8, 2 * WIN))
    row = lax.broadcasted_iota(jnp.int32, (8, WIN), 0)
    out[0, BLK:, :] = jnp.where(
        row == 0, low_half(norms[:, :WIN], odd), low_half(norms[:, WIN:], other_odd)
    )


def gram(sources, arrive, order):
    groups, rows = len(sources), sources[0].shape[0]
    pairs = arrive.shape[0] // 2
    return pl.pallas_call(
        functools.partial(gram_kernel, groups),
        grid_spec=pltpu.PrefetchScalarGridSpec(
            num_scalar_prefetch=2,
            grid=(pairs,),
            in_specs=[pl.BlockSpec(memory_space=pl.ANY)] * groups,
            out_specs=pl.BlockSpec((1, BLK + 8, WIN), lambda q, *_: (q, 0, 0)),
            scratch_shapes=[
                pltpu.VMEM((2, 2, rows, WIN), jnp.float32),
                pltpu.SemaphoreType.DMA((2, 2)),
            ],
        ),
        out_shape=jax.ShapeDtypeStruct((pairs, BLK + 8, WIN), jnp.float32),
        compiler_params=pltpu.CompilerParams(vmem_limit_bytes=VMEM_LIMIT),
        cost_estimate=pl.CostEstimate(
            flops=6 * pairs * rows * WIN * WIN,
            bytes_accessed=8 * pairs * rows * WIN,
            transcendentals=0,
        ),
        name="cross_products",
    )(arrive, order, *sources)


def rotate_kernel(groups, row0, given, arrive, order, *refs):
    sources, turn = refs[:groups], refs[groups]
    out, win, sems = refs[groups + 1 + given :]
    rows = win.shape[2]
    q, slot = pipelined(*fetcher(arrive, order, sources, win, sems, row0, rows))
    tile = tile_of(rows)
    long_turn = long_halves(spread(turn[0], order[2 * q] % 2, order[2 * q + 1] % 2))
    for step in range(rows // tile):
        x = pair_tile(win, slot, step * tile, tile)
        out[step * tile : (step + 1) * tile, :] = turned_tile(x, long_turn)


def rotate(sources, arrive, order, turns, row0, rows, into=None, shape=None, at=0):
    groups = len(sources)
    pairs = arrive.shape[0] // 2
    shape = shape or (rows, pairs * 2 * BLK)
    given = [] if into is None else [into]
    return pl.pallas_call(
        functools.partial(rotate_kernel, groups, row0, len(given)),
        grid_spec=pltpu.PrefetchScalarGridSpec(
            num_scalar_prefetch=2,
            grid=(pairs,),
            in_specs=[pl.BlockSpec(memory_space=pl.ANY)] * groups
            + [pl.BlockSpec((1, 2 * BLK, 2 * BLK), lambda q, *_: (q, 0, 0))]
            + [pl.BlockSpec(memory_space=pl.ANY)] * len(given),
            out_specs=pl.BlockSpec((rows, 2 * BLK), lambda q, *_: (at, q)),
            scratch_shapes=[
                pltpu.VMEM((2, 2, rows, WIN), jnp.float32),
                pltpu.SemaphoreType.DMA((2, 2)),
            ],
        ),
        out_shape=jax.ShapeDtypeStruct(shape, jnp.float32),
        input_output_aliases={groups + 3: 0} if given else {},
        compiler_params=pltpu.CompilerParams(vmem_limit_bytes=VMEM_LIMIT),
        cost_estimate=pl.CostEstimate(
            flops=6 * pairs * rows * 4 * BLK * BLK,
            bytes_accessed=4 * pairs * rows * (2 * WIN + 2 * BLK),
            transcendentals=0,
        ),
        name="rotate",
    )(arrive, order, *sources, turns, *given)


def gather_kernel(rows_at, x_ref, out):
    out[0] = x_ref[...]


def gather_rows(x, rows_at):
    count = rows_at.shape[0]
    return pl.pallas_call(
        gather_kernel,
        grid_spec=pltpu.PrefetchScalarGridSpec(
            num_scalar_prefetch=1,
            grid=(count,),
            in_specs=[pl.BlockSpec((ROWB, x.shape[1]), lambda i, at: (at[i], 0))],
            out_specs=pl.BlockSpec((1, ROWB, x.shape[1]), lambda i, at: (i, 0, 0)),
        ),
        out_shape=jax.ShapeDtypeStruct((count, ROWB, x.shape[1]), jnp.float32),
        compiler_params=pltpu.CompilerParams(vmem_limit_bytes=VMEM_LIMIT),
        cost_estimate=pl.CostEstimate(
            flops=0, bytes_accessed=8 * count * ROWB * x.shape[1], transcendentals=0
        ),
        name="gather_rows",
    )(rows_at, x)


def slab_pack_kernel(groups, *refs):
    sources, (out, held, in_sems, out_sems) = refs[:groups], refs[groups:]
    slabs, rows, _ = out.shape
    width = sources[0].shape[1]
    arrivals = []
    for o in range(slabs):
        for g in range(groups):
            copy = pltpu.make_async_copy(
                sources[g].at[pl.ds(o * rows, rows), :],
                held.at[o, :, pl.ds(g * width, width)],
                in_sems.at[o, g],
            )
            copy.start()
            arrivals.append(copy)
    departures = []
    for o in range(slabs):
        for copy in arrivals[o * groups : (o + 1) * groups]:
            copy.wait()
        copy = pltpu.make_async_copy(held.at[o], out.at[o], out_sems.at[o])
        copy.start()
        departures.append(copy)
    for copy in departures:
        copy.wait()


def slab_pack(sources, slabs):
    groups = len(sources)
    rows, width = sources[0].shape[0] // slabs, sources[0].shape[1]
    shape = (slabs, rows, groups * width)
    return pl.pallas_call(
        functools.partial(slab_pack_kernel, groups),
        in_specs=[pl.BlockSpec(memory_space=pl.ANY)] * groups,
        out_specs=pl.BlockSpec(memory_space=pl.ANY),
        scratch_shapes=[
            pltpu.VMEM(shape, jnp.float32),
            pltpu.SemaphoreType.DMA((slabs, groups)),
            pltpu.SemaphoreType.DMA((slabs,)),
        ],
        out_shape=jax.ShapeDtypeStruct(shape, jnp.float32),
        compiler_params=pltpu.CompilerParams(vmem_limit_bytes=VMEM_LIMIT),
        cost_estimate=pl.CostEstimate(
            flops=0, bytes_accessed=8 * slabs * rows * groups * width, transcendentals=0
        ),
        name="slab_pack",
    )(*sources)


def settle_kernel(groups, strips, given, arrive, order, natural, *refs):
    sources, turn = refs[:groups], refs[groups]
    out, win, done, sems, out_sems = refs[groups + 1 + given :]
    rows = win.shape[2]
    if groups == 1:
        source = sources[0]

        def start(q, slot):
            for side in range(2):
                strip = arrive[2 * q + side] * strips + (3 * order[2 * q + side]) // 2
                pltpu.make_async_copy(
                    source.at[:, pl.ds(pl.multiple_of(strip * 128, 128), WIN)],
                    win.at[slot, side],
                    sems.at[slot, side],
                ).start()

        _, wait = fetcher(arrive, order, sources, win, sems, 0, rows)
    else:
        start, wait = fetcher(arrive, order, sources, win, sems, 0, rows)

    q, slot = pipelined(start, wait)
    tile = tile_of(rows)
    long_turn = long_halves(spread(turn[0], order[2 * q] % 2, order[2 * q + 1] % 2))

    def written(at):
        pltpu.make_async_copy(done.at[at], done.at[at], out_sems.at[at]).wait()

    @pl.when(q >= 2)
    def _():
        written(slot)

    for step in range(rows // tile):
        x = pair_tile(win, slot, step * tile, tile)
        done[slot, step * tile : (step + 1) * tile, :] = turned_tile(x, long_turn)

    columns = pl.ds(pl.multiple_of(q * 2 * BLK, 128), 2 * BLK)
    for block in range(rows // ROWB):
        pltpu.make_async_copy(
            done.at[slot, pl.ds(block * ROWB, ROWB), :],
            out.at[pl.ds(pl.multiple_of(natural[block] * ROWB, 8), ROWB), columns],
            out_sems.at[slot],
        ).start()

    @pl.when(q == pl.num_programs(0) - 1)
    def _():
        written(slot)

        @pl.when(q >= 1)
        def _():
            written(1 - slot)


def settle(sources, arrive, order, natural, turns, strips, shape, into=None):
    groups, rows = len(sources), sources[0].shape[0]
    pairs = arrive.shape[0] // 2
    given = [] if into is None else [into]
    return pl.pallas_call(
        functools.partial(settle_kernel, groups, strips, len(given)),
        grid_spec=pltpu.PrefetchScalarGridSpec(
            num_scalar_prefetch=3,
            grid=(pairs,),
            in_specs=[pl.BlockSpec(memory_space=pl.ANY)] * groups
            + [pl.BlockSpec((1, 2 * BLK, 2 * BLK), lambda q, *_: (q, 0, 0))]
            + [pl.BlockSpec(memory_space=pl.ANY)] * len(given),
            out_specs=pl.BlockSpec(memory_space=pl.ANY),
            scratch_shapes=[
                pltpu.VMEM((2, 2, rows, WIN), jnp.float32),
                pltpu.VMEM((2, rows, 2 * BLK), jnp.float32),
                pltpu.SemaphoreType.DMA((2, 2)),
                pltpu.SemaphoreType.DMA((2,)),
            ],
        ),
        out_shape=jax.ShapeDtypeStruct(shape, jnp.float32),
        input_output_aliases={groups + 4: 0} if given else {},
        compiler_params=pltpu.CompilerParams(vmem_limit_bytes=VMEM_LIMIT),
        cost_estimate=pl.CostEstimate(
            flops=6 * pairs * rows * 4 * BLK * BLK,
            bytes_accessed=4 * pairs * rows * (2 * WIN + 2 * BLK),
            transcendentals=0,
        ),
        name="settle",
    )(arrive, order, natural, *sources, turns, *given)


def swap(arrays, axis):
    count = len(arrays)
    return [arrays[0]] + [
        lax.ppermute(arrays[o], axis, [(i, i ^ o) for i in range(count)]) for o in range(1, count)
    ]


def after(arrays, earlier):
    return lax.optimization_barrier((arrays, earlier))


def shards(groups, slabs, r_slabs, basis, owners, plan):
    rows = r_slabs.shape[0]
    count = r_slabs.shape[1] // BLK
    units = count // groups
    strips = unit_width(units) // 128
    row_blocks = owners.shape[0]
    each = row_blocks // slabs
    early = 1 if each > 1 else 0
    late = each - early
    late_cuts = [1, late - 1] if late > 1 else [late]
    part = rows // 2
    pair_index = lax.axis_index("pair")
    slab_index = lax.axis_index("slab")

    send_0, arrive_0, order_0 = move_tables(plan[0], pair_index, groups, count)
    slot_ids = jnp.arange(plan.shape[1], dtype=jnp.int32)
    place_1 = jnp.sum(
        jnp.where(plan[0][None, :] == plan[1][:, None], slot_ids[None, :], 0), axis=1
    )
    send_1, arrive_1, order_1 = move_tables(place_1, pair_index, groups, count)

    goes_to = owners // row_blocks
    rank = rank_among(goes_to)
    bounds, low = [], 0
    for size in [early] * (early > 0) + late_cuts:
        bounds.append((low, low + size))
        low += size
    spot = sum(
        jnp.where(
            (rank >= lo) & (rank < hi), slabs * lo + goes_to * (hi - lo) + rank - lo, 0
        )
        for lo, hi in bounds
    )
    index = jnp.arange(row_blocks, dtype=jnp.int32)
    rows_at = jnp.sum(jnp.where(spot[None, :] == index[:, None], index[None, :], 0), axis=1)
    table = lax.all_gather(owners, "slab", axis=0, tiled=True).reshape(slabs, row_blocks)
    table_to = table // row_blocks
    table_rank = rank_among(table_to)
    per_rank = jnp.arange(each, dtype=jnp.int32)
    hit = (table_to == slab_index)[:, None, :] & (table_rank[:, None, :] == per_rank[None, :, None])
    where_to = jnp.sum(jnp.where(hit, (table % row_blocks)[:, None, :], 0), axis=2)
    natural = [where_to[:, lo:hi].reshape(slabs * (hi - lo)) for lo, hi in bounds]

    def straight(size, start=0):
        return jnp.arange(size // ROWB, dtype=jnp.int32) + start // ROWB

    def over_slab(blocks):
        return lax.all_to_all(blocks, "slab", 0, 0, tiled=True)

    r_sent = pack(r_slabs, send_0, rows_at[slabs * early :], ROWB, groups, units)
    send_v, r_sent = after(send_0, r_sent)
    r_late = swap(r_sent, "pair")
    first = []
    if early:
        (rows_early,), r_sent = after([rows_at[: slabs * early]], r_sent)
        home = over_slab(gather_rows(r_slabs, rows_early)).reshape(-1, r_slabs.shape[1])
        sent = pack(home, send_0, straight(home.shape[0]), ROWB, groups, units)
        sent, (r_late, natural) = after(sent, (r_late, natural))
        first.append(swap(sent, "pair"))
    first.append(r_late)
    grams = [gram(got, arrive_0, order_0) for got in first]

    v_sent = [
        pack(basis, send_v, straight(part, c * part), ROWB, groups, units) for c in range(2)
    ]
    v_sent[0], (first[0], grams[1:], natural) = after(
        v_sent[0], (first[0], grams[1:], natural)
    )
    if early:
        grams[0] = gram(first[0], arrive_0, order_0)
    v_got = [swap(v_sent[0], "pair"), None]
    turns = turns_of(lax.psum(functools.reduce(jnp.add, grams), "slab"))

    def second(sources, row0, size):
        turned = rotate(sources, arrive_0, order_0, turns, row0, size)
        return pack(turned, send_1, straight(size), ROWB, groups, units)

    late_chunks, row0 = [], 0
    for lo, hi in bounds[1 if early else 0 :]:
        size = (hi - lo) * slabs * ROWB
        late_chunks.append((first[-1], row0, size))
        row0 += size
    early_chunks = [(first[0], 0, early * slabs * ROWB)] if early else []
    r_two, last = [], v_got[0]
    for sources, row0, size in late_chunks + early_chunks:
        sent = second(sources, row0, size)
        sent, last = after(sent, last)
        if r_two:
            r_two[-1] = last
        else:
            v_got[0] = last
        last = swap(sent, "pair")
        r_two.append(last)

    packed = [slab_pack(r_two[c], slabs) for c in range(len(late_chunks))]
    v_sent[1], r_two[-1] = after(v_sent[1], r_two[-1])
    v_got[1] = swap(v_sent[1], "pair")
    r_home = [over_slab(blocks) for blocks in packed]
    sums = functools.reduce(jnp.add, [gram(got, arrive_1, order_1) for got in r_two])
    v_got[0], sums = after(v_got[0], sums)
    sums = lax.psum(sums, "slab")

    v_next, v_got[1] = after(second(v_got[0], 0, part), v_got[1])
    v_two = [swap(v_next, "pair")]
    (v_next, sums), v_two[0] = after((second(v_got[1], 0, part), sums), v_two[0])
    v_two.append(swap(v_next, "pair"))
    turns_1 = turns_of(sums)

    v_out = rotate(v_two[0], arrive_1, order_1, turns_1, 0, part, None, basis.shape, 0)
    r_out = None
    if early:
        r_out = settle(
            r_two[-1], arrive_1, order_1, natural[0], turns_1, strips, r_slabs.shape
        )
    for c, blocks in enumerate(r_home):
        r_out = settle(
            [blocks.reshape(-1, blocks.shape[2])],
            arrive_1,
            order_1,
            natural[c + early],
            turns_1,
            strips,
            r_slabs.shape,
            r_out,
        )
    v_two[1], (r_out, v_out) = after(v_two[1], (r_out, v_out))
    v_out = rotate(v_two[1], arrive_1, order_1, turns_1, 0, part, v_out, basis.shape, 1)
    return r_out, v_out


def solution(mesh):
    placed = (P("slab", "pair"), P("slab", "pair"), P("slab"), P())
    return jax.shard_map(
        functools.partial(shards, mesh.shape["pair"], mesh.shape["slab"]),
        mesh=mesh,
        in_specs=placed,
        out_specs=(P("slab", "pair"), P("slab", "pair")),
        check_vma=False,
    )
```

```python
import functools

import jax
import jax.numpy as jnp
from jax import lax
from jax.experimental import pallas as pl
from jax.experimental.pallas import tpu as pltpu
from jax.sharding import PartitionSpec as P

BLK = 192
ROWB = 48
WIN = 256
EPSILON = 1e-06
HIGH = lax.Precision.HIGH
VMEM_LIMIT = 48 * 1024 * 1024


def rotations(cross_gram, norms_a, norms_b):
    width = cross_gram.shape[-1]
    scale_a = lax.rsqrt(norms_a)
    scale_b = lax.rsqrt(norms_b)
    normed = cross_gram * scale_a[:, :, None] * scale_b[:, None, :]
    frobenius = jnp.sqrt(jnp.sum(normed * normed, axis=(1, 2)))
    coupling = normed / (1.0 + frobenius)[:, None, None]
    outer_a = jnp.einsum("pik,pjk->pij", coupling, coupling, precision=HIGH)
    outer_b = jnp.einsum("pki,pkj->pij", coupling, coupling, precision=HIGH)
    identity = jnp.eye(width, dtype=cross_gram.dtype)
    left_poly = (
        identity
        - 0.5 * outer_a
        + 0.375 * jnp.einsum("pik,pkj->pij", outer_a, outer_a, precision=HIGH)
    )
    right_poly = (
        identity
        - 0.5 * outer_b
        + 0.375 * jnp.einsum("pik,pkj->pij", outer_b, outer_b, precision=HIGH)
    )
    upper_half = jnp.concatenate(
        [left_poly, -jnp.einsum("pik,pkj->pij", coupling, right_poly, precision=HIGH)], axis=2
    )
    lower_half = jnp.concatenate(
        [jnp.einsum("pki,pkj->pij", coupling, left_poly, precision=HIGH), right_poly], axis=2
    )
    return jnp.concatenate([upper_half, lower_half], axis=1)


def turns_of(sums):
    cross_gram = sums[:, :BLK, :BLK]
    norms_a = sums[:, BLK, :BLK] + EPSILON
    norms_b = sums[:, BLK + 1, :BLK] + EPSILON
    return rotations(cross_gram, norms_a, norms_b)


def move_tables(place, me, groups, count):
    total = place.shape[0]
    units = count // groups
    slots = jnp.arange(total, dtype=jnp.int32)
    source, local = place // count, place % count
    target = slots // count
    same = (target[:, None] == target[None, :]) & (source[:, None] == source[None, :])
    rank = jnp.sum((same & (slots[None, :] < slots[:, None])).astype(jnp.int32), axis=1)
    offset = jnp.arange(groups, dtype=jnp.int32)
    unit = jnp.arange(units, dtype=jnp.int32)
    chosen = (
        (source == me)[None, None, :]
        & (target[None, None, :] == (me ^ offset)[:, None, None])
        & (rank[None, None, :] == unit[None, :, None])
    )
    send = jnp.sum(jnp.where(chosen, local[None, None, :], 0), axis=2).reshape(groups * units)
    mine = lax.dynamic_slice_in_dim(source ^ me, me * count, count)
    order = lax.dynamic_slice_in_dim(rank, me * count, count)
    return send, mine, order


def rank_among(kind):
    index = jnp.arange(kind.shape[-1], dtype=jnp.int32)
    same = (kind[..., :, None] == kind[..., None, :]) & (index[None, :] < index[:, None])
    return jnp.sum(same.astype(jnp.int32), axis=-1)


def shifted(window, left):
    return pltpu.roll(window, WIN - 64 if left else 64, 1)


def low_half(window, odd):
    return jnp.where(odd == 1, shifted(window, True), window)


def merge(first, first_odd, second, second_odd):
    a = low_half(first, first_odd)
    b = jnp.where(second_odd == 1, second, shifted(second, False))
    lane = lax.broadcasted_iota(jnp.int32, (first.shape[0], 128), 1)
    middle = jnp.where(lane < 64, a[:, 128:], b[:, :128])
    return jnp.concatenate([a[:, :128], middle, b[:, 128:]], axis=1)


def unit_width(units):
    return max(WIN, units * BLK)


def pack_kernel(groups, units, blocks, send, rows_at, *refs):
    sources, outs = refs[:blocks], refs[blocks:]
    size = sources[0].shape[0]
    for i, x_ref in enumerate(sources):
        rows = slice(i * size, (i + 1) * size)

        def window(place):
            block = send[place]
            strip = (3 * block) // 2
            return x_ref[:, pl.ds(pl.multiple_of(strip * 128, 128), WIN)], block % 2

        for group in range(groups):
            if units == 1:
                w, odd = window(group)
                outs[group][rows, :] = low_half(w, odd)
            for j in range(0, units - 1, 2):
                w0, odd0 = window(group * units + j)
                w1, odd1 = window(group * units + j + 1)
                outs[group][rows, BLK * j : BLK * (j + 2)] = merge(w0, odd0, w1, odd1)


def pack(x, send, rows_at, block_rows, groups, units):
    total = rows_at.shape[0]
    blocks = 4 if total % 4 == 0 else 1
    width = unit_width(units)

    def block_at(k):
        return pl.BlockSpec(
            (block_rows, x.shape[1]), lambda i, send, at: (at[i * blocks + k], 0)
        )

    return pl.pallas_call(
        functools.partial(pack_kernel, groups, units, blocks),
        grid_spec=pltpu.PrefetchScalarGridSpec(
            num_scalar_prefetch=2,
            grid=(total // blocks,),
            in_specs=[block_at(k) for k in range(blocks)],
            out_specs=[pl.BlockSpec((blocks * block_rows, width), lambda i, *_: (i, 0))]
            * groups,
        ),
        out_shape=[jax.ShapeDtypeStruct((total * block_rows, width), jnp.float32)] * groups,
        compiler_params=pltpu.CompilerParams(vmem_limit_bytes=VMEM_LIMIT),
        cost_estimate=pl.CostEstimate(
            flops=0,
            bytes_accessed=2 * 4 * total * block_rows * x.shape[1],
            transcendentals=0,
        ),
        name="pack",
    )(send, rows_at, *[x] * blocks)


def halves(x):
    high = x.astype(jnp.bfloat16)
    return high, (x - high.astype(jnp.float32)).astype(jnp.bfloat16)


def product(a, b, dims):
    (ah, al), (bh, bl) = a, b
    dot = functools.partial(
        lax.dot_general, dimension_numbers=(dims, ((), ())), preferred_element_type=jnp.float32
    )
    return dot(ah, bh) + (dot(al, bh) + dot(ah, bl))


def fetcher(arrive, order, sources, win, sems, row0, rows):
    def start(q, slot):
        for side in range(2):
            at = arrive[2 * q + side]
            strip = (3 * order[2 * q + side]) // 2
            for k, source in enumerate(sources):

                @pl.when(at == k)
                def _():
                    pltpu.make_async_copy(
                        source.at[
                            pl.ds(row0, rows), pl.ds(pl.multiple_of(strip * 128, 128), WIN)
                        ],
                        win.at[slot, side],
                        sems.at[slot, side],
                    ).start()

    def wait(slot):
        for side in range(2):
            pltpu.make_async_copy(
                sources[0].at[pl.ds(row0, rows), pl.ds(0, WIN)],
                win.at[slot, side],
                sems.at[slot, side],
            ).wait()

    return start, wait


def pipelined(start, wait):
    q, last = pl.program_id(0), pl.num_programs(0)
    slot = lax.rem(q, 2)

    @pl.when(q == 0)
    def _():
        start(0, 0)

    @pl.when(q + 1 < last)
    def _():
        start(q + 1, 1 - slot)

    wait(slot)
    return q, slot


def tile_of(rows):
    return 384 if rows % 384 == 0 else rows


def pair_tile(win, slot, start, tile):
    rows = pl.ds(pl.multiple_of(start, 8), tile)
    return jnp.concatenate([win[slot, 0, rows, :], win[slot, 1, rows, :]], axis=1)


def spread(turn, odd, other_odd):
    gap = jnp.zeros((WIN - BLK, 2 * BLK), jnp.float32)

    def placed(part, odd):
        return jnp.where(
            odd == 1, jnp.concatenate([gap, part]), jnp.concatenate([part, gap])
        )

    return jnp.concatenate([placed(turn[:BLK], odd), placed(turn[BLK:], other_odd)])


def long_halves(turn):
    high, low = halves(turn)
    return jnp.concatenate([high, high, low])


def turned_tile(x, long_turn):
    high, low = halves(x)
    return jnp.dot(
        jnp.concatenate([high, low, high], axis=1), long_turn, preferred_element_type=jnp.float32
    )


def gram_kernel(groups, given, arrive, order, *refs):
    sources, earlier = refs[:groups], refs[groups : groups + given]
    out, win, sems = refs[groups + given :]
    rows = win.shape[2]
    q, slot = pipelined(*fetcher(arrive, order, sources, win, sems, 0, rows))
    tile = tile_of(rows)
    total = jnp.zeros((WIN, WIN), jnp.float32)
    squares = jnp.zeros((8, 2 * WIN), jnp.float32)
    for step in range(rows // tile):
        x = pair_tile(win, slot, step * tile, tile)
        high, low = halves(x)
        total += product(
            (high[:, :WIN], low[:, :WIN]), (high[:, WIN:], low[:, WIN:]), ((0,), (0,))
        )
        squares += jnp.sum((x * x).reshape(tile // 8, 8, 2 * WIN), axis=0)
    odd, other_odd = order[2 * q] % 2, order[2 * q + 1] % 2
    total = jnp.where(odd == 1, total[WIN - BLK :], total[:BLK])
    out[0, :BLK, :] = low_half(total, other_odd)
    norms = jnp.broadcast_to(jnp.sum(squares, axis=0, keepdims=True), (8, 2 * WIN))
    row = lax.broadcasted_iota(jnp.int32, (8, WIN), 0)
    out[0, BLK:, :] = jnp.where(
        row == 0, low_half(norms[:, :WIN], odd), low_half(norms[:, WIN:], other_odd)
    )
    for sums in earlier:
        out[...] += sums[...]


def gram(sources, arrive, order, earlier=None):
    groups, rows = len(sources), sources[0].shape[0]
    given = [] if earlier is None else [earlier]
    sums = pl.BlockSpec((1, BLK + 8, WIN), lambda q, *_: (q, 0, 0))
    pairs = arrive.shape[0] // 2
    return pl.pallas_call(
        functools.partial(gram_kernel, groups, len(given)),
        grid_spec=pltpu.PrefetchScalarGridSpec(
            num_scalar_prefetch=2,
            grid=(pairs,),
            in_specs=[pl.BlockSpec(memory_space=pl.ANY)] * groups + [sums] * len(given),
            out_specs=sums,
            scratch_shapes=[
                pltpu.VMEM((2, 2, rows, WIN), jnp.float32),
                pltpu.SemaphoreType.DMA((2, 2)),
            ],
        ),
        out_shape=jax.ShapeDtypeStruct((pairs, BLK + 8, WIN), jnp.float32),
        compiler_params=pltpu.CompilerParams(vmem_limit_bytes=VMEM_LIMIT),
        cost_estimate=pl.CostEstimate(
            flops=6 * pairs * rows * WIN * WIN,
            bytes_accessed=8 * pairs * rows * WIN,
            transcendentals=0,
        ),
        name="cross_products",
    )(arrive, order, *sources, *given)


def rotate_kernel(groups, row0, given, arrive, order, *refs):
    sources, turn = refs[:groups], refs[groups]
    out, win, sems = refs[groups + 1 + given :]
    rows = win.shape[2]
    q, slot = pipelined(*fetcher(arrive, order, sources, win, sems, row0, rows))
    tile = tile_of(rows)
    long_turn = long_halves(spread(turn[0], order[2 * q] % 2, order[2 * q + 1] % 2))
    for step in range(rows // tile):
        x = pair_tile(win, slot, step * tile, tile)
        out[step * tile : (step + 1) * tile, :] = turned_tile(x, long_turn)


def rotate(sources, arrive, order, turns, row0, rows, into=None, shape=None, at=0):
    groups = len(sources)
    pairs = arrive.shape[0] // 2
    shape = shape or (rows, pairs * 2 * BLK)
    given = [] if into is None else [into]
    return pl.pallas_call(
        functools.partial(rotate_kernel, groups, row0, len(given)),
        grid_spec=pltpu.PrefetchScalarGridSpec(
            num_scalar_prefetch=2,
            grid=(pairs,),
            in_specs=[pl.BlockSpec(memory_space=pl.ANY)] * groups
            + [pl.BlockSpec((1, 2 * BLK, 2 * BLK), lambda q, *_: (q, 0, 0))]
            + [pl.BlockSpec(memory_space=pl.ANY)] * len(given),
            out_specs=pl.BlockSpec((rows, 2 * BLK), lambda q, *_: (at, q)),
            scratch_shapes=[
                pltpu.VMEM((2, 2, rows, WIN), jnp.float32),
                pltpu.SemaphoreType.DMA((2, 2)),
            ],
        ),
        out_shape=jax.ShapeDtypeStruct(shape, jnp.float32),
        input_output_aliases={groups + 3: 0} if given else {},
        compiler_params=pltpu.CompilerParams(vmem_limit_bytes=VMEM_LIMIT),
        cost_estimate=pl.CostEstimate(
            flops=6 * pairs * rows * 4 * BLK * BLK,
            bytes_accessed=4 * pairs * rows * (2 * WIN + 2 * BLK),
            transcendentals=0,
        ),
        name="rotate",
    )(arrive, order, *sources, turns, *given)


def gather_kernel(rows_at, x_ref, out, held, in_sems, out_sems):
    count = out.shape[0]

    def arrival(i):
        start = pl.multiple_of(rows_at[i] * ROWB, 8)
        return pltpu.make_async_copy(
            x_ref.at[pl.ds(start, ROWB), :], held.at[i], in_sems.at[i]
        )

    def departure(i):
        return pltpu.make_async_copy(held.at[i], out.at[i], out_sems.at[i])

    for i in range(count):
        arrival(i).start()
    for i in range(count):
        arrival(i).wait()
        departure(i).start()
    for i in range(count):
        departure(i).wait()


def gather_rows(x, rows_at):
    count = rows_at.shape[0]
    shape = (count, ROWB, x.shape[1])
    return pl.pallas_call(
        gather_kernel,
        grid_spec=pltpu.PrefetchScalarGridSpec(
            num_scalar_prefetch=1,
            grid=(1,),
            in_specs=[pl.BlockSpec(memory_space=pl.ANY)],
            out_specs=pl.BlockSpec(memory_space=pl.ANY),
            scratch_shapes=[
                pltpu.VMEM(shape, jnp.float32),
                pltpu.SemaphoreType.DMA((count,)),
                pltpu.SemaphoreType.DMA((count,)),
            ],
        ),
        out_shape=jax.ShapeDtypeStruct(shape, jnp.float32),
        compiler_params=pltpu.CompilerParams(vmem_limit_bytes=VMEM_LIMIT),
        cost_estimate=pl.CostEstimate(
            flops=0, bytes_accessed=8 * count * ROWB * x.shape[1], transcendentals=0
        ),
        name="gather_rows",
    )(rows_at, x)


def slab_pack_kernel(groups, *refs):
    sources, (out, held, in_sems, out_sems) = refs[:groups], refs[groups:]
    slabs, rows, _ = out.shape
    width = sources[0].shape[1]
    arrivals = []
    for o in range(slabs):
        for g in range(groups):
            copy = pltpu.make_async_copy(
                sources[g].at[pl.ds(o * rows, rows), :],
                held.at[o, :, pl.ds(g * width, width)],
                in_sems.at[o, g],
            )
            copy.start()
            arrivals.append(copy)
    departures = []
    for o in range(slabs):
        for copy in arrivals[o * groups : (o + 1) * groups]:
            copy.wait()
        copy = pltpu.make_async_copy(held.at[o], out.at[o], out_sems.at[o])
        copy.start()
        departures.append(copy)
    for copy in departures:
        copy.wait()


def slab_pack(sources, slabs):
    groups = len(sources)
    rows, width = sources[0].shape[0] // slabs, sources[0].shape[1]
    shape = (slabs, rows, groups * width)
    return pl.pallas_call(
        functools.partial(slab_pack_kernel, groups),
        in_specs=[pl.BlockSpec(memory_space=pl.ANY)] * groups,
        out_specs=pl.BlockSpec(memory_space=pl.ANY),
        scratch_shapes=[
            pltpu.VMEM(shape, jnp.float32),
            pltpu.SemaphoreType.DMA((slabs, groups)),
            pltpu.SemaphoreType.DMA((slabs,)),
        ],
        out_shape=jax.ShapeDtypeStruct(shape, jnp.float32),
        compiler_params=pltpu.CompilerParams(vmem_limit_bytes=VMEM_LIMIT),
        cost_estimate=pl.CostEstimate(
            flops=0, bytes_accessed=8 * slabs * rows * groups * width, transcendentals=0
        ),
        name="slab_pack",
    )(*sources)


def settle_kernel(groups, strips, given, arrive, order, natural, *refs):
    sources, turn = refs[:groups], refs[groups]
    out, win, done, sems, out_sems = refs[groups + 1 + given :]
    rows = win.shape[2]
    if groups == 1:
        source = sources[0]

        def start(q, slot):
            for side in range(2):
                strip = arrive[2 * q + side] * strips + (3 * order[2 * q + side]) // 2
                pltpu.make_async_copy(
                    source.at[:, pl.ds(pl.multiple_of(strip * 128, 128), WIN)],
                    win.at[slot, side],
                    sems.at[slot, side],
                ).start()

        _, wait = fetcher(arrive, order, sources, win, sems, 0, rows)
    else:
        start, wait = fetcher(arrive, order, sources, win, sems, 0, rows)

    q, slot = pipelined(start, wait)
    tile = tile_of(rows)
    long_turn = long_halves(spread(turn[0], order[2 * q] % 2, order[2 * q + 1] % 2))

    def written(at):
        pltpu.make_async_copy(done.at[at], done.at[at], out_sems.at[at]).wait()

    @pl.when(q >= 2)
    def _():
        written(slot)

    for step in range(rows // tile):
        x = pair_tile(win, slot, step * tile, tile)
        done[slot, step * tile : (step + 1) * tile, :] = turned_tile(x, long_turn)

    columns = pl.ds(pl.multiple_of(q * 2 * BLK, 128), 2 * BLK)
    for block in range(rows // ROWB):
        pltpu.make_async_copy(
            done.at[slot, pl.ds(block * ROWB, ROWB), :],
            out.at[pl.ds(pl.multiple_of(natural[block] * ROWB, 8), ROWB), columns],
            out_sems.at[slot],
        ).start()

    @pl.when(q == pl.num_programs(0) - 1)
    def _():
        written(slot)

        @pl.when(q >= 1)
        def _():
            written(1 - slot)


def settle(sources, arrive, order, natural, turns, strips, shape, into=None):
    groups, rows = len(sources), sources[0].shape[0]
    pairs = arrive.shape[0] // 2
    given = [] if into is None else [into]
    return pl.pallas_call(
        functools.partial(settle_kernel, groups, strips, len(given)),
        grid_spec=pltpu.PrefetchScalarGridSpec(
            num_scalar_prefetch=3,
            grid=(pairs,),
            in_specs=[pl.BlockSpec(memory_space=pl.ANY)] * groups
            + [pl.BlockSpec((1, 2 * BLK, 2 * BLK), lambda q, *_: (q, 0, 0))]
            + [pl.BlockSpec(memory_space=pl.ANY)] * len(given),
            out_specs=pl.BlockSpec(memory_space=pl.ANY),
            scratch_shapes=[
                pltpu.VMEM((2, 2, rows, WIN), jnp.float32),
                pltpu.VMEM((2, rows, 2 * BLK), jnp.float32),
                pltpu.SemaphoreType.DMA((2, 2)),
                pltpu.SemaphoreType.DMA((2,)),
            ],
        ),
        out_shape=jax.ShapeDtypeStruct(shape, jnp.float32),
        input_output_aliases={groups + 4: 0} if given else {},
        compiler_params=pltpu.CompilerParams(vmem_limit_bytes=VMEM_LIMIT),
        cost_estimate=pl.CostEstimate(
            flops=6 * pairs * rows * 4 * BLK * BLK,
            bytes_accessed=4 * pairs * rows * (2 * WIN + 2 * BLK),
            transcendentals=0,
        ),
        name="settle",
    )(arrive, order, natural, *sources, turns, *given)


def swap(arrays, axis):
    count = len(arrays)
    return [arrays[0]] + [
        lax.ppermute(arrays[o], axis, [(i, i ^ o) for i in range(count)]) for o in range(1, count)
    ]


def after(arrays, earlier):
    return lax.optimization_barrier((arrays, earlier))


def shards(groups, slabs, r_slabs, basis, owners, plan):
    rows = r_slabs.shape[0]
    count = r_slabs.shape[1] // BLK
    units = count // groups
    strips = unit_width(units) // 128
    row_blocks = owners.shape[0]
    each = row_blocks // slabs
    early = 1 if each > 1 else 0
    late = each - early
    late_cuts = [1, late - 1] if late > 1 else [late]
    part = rows // 2
    pair_index = lax.axis_index("pair")
    slab_index = lax.axis_index("slab")

    send_0, arrive_0, order_0 = move_tables(plan[0], pair_index, groups, count)
    slot_ids = jnp.arange(plan.shape[1], dtype=jnp.int32)
    place_1 = jnp.sum(
        jnp.where(plan[0][None, :] == plan[1][:, None], slot_ids[None, :], 0), axis=1
    )
    send_1, arrive_1, order_1 = move_tables(place_1, pair_index, groups, count)

    goes_to = owners // row_blocks
    rank = rank_among(goes_to)
    bounds, low = [], 0
    for size in [early] * (early > 0) + late_cuts:
        bounds.append((low, low + size))
        low += size
    spot = sum(
        jnp.where(
            (rank >= lo) & (rank < hi), slabs * lo + goes_to * (hi - lo) + rank - lo, 0
        )
        for lo, hi in bounds
    )
    index = jnp.arange(row_blocks, dtype=jnp.int32)
    rows_at = jnp.sum(jnp.where(spot[None, :] == index[:, None], index[None, :], 0), axis=1)
    table = lax.all_gather(owners, "slab", axis=0, tiled=True).reshape(slabs, row_blocks)
    table_to = table // row_blocks
    table_rank = rank_among(table_to)
    per_rank = jnp.arange(each, dtype=jnp.int32)
    hit = (table_to == slab_index)[:, None, :] & (table_rank[:, None, :] == per_rank[None, :, None])
    where_to = jnp.sum(jnp.where(hit, (table % row_blocks)[:, None, :], 0), axis=2)
    natural = [where_to[:, lo:hi].reshape(slabs * (hi - lo)) for lo, hi in bounds]

    def straight(size, start=0):
        return jnp.arange(size // ROWB, dtype=jnp.int32) + start // ROWB

    def over_slab(blocks):
        return lax.all_to_all(blocks, "slab", 0, 0, tiled=True)

    r_sent = pack(r_slabs, send_0, rows_at[slabs * early :], ROWB, groups, units)
    send_v, r_sent = after(send_0, r_sent)
    r_late = swap(r_sent, "pair")
    first = []
    if early:
        (rows_early,), r_sent = after([rows_at[: slabs * early]], r_sent)
        home = over_slab(gather_rows(r_slabs, rows_early)).reshape(-1, r_slabs.shape[1])
        sent = pack(home, send_0, straight(home.shape[0]), ROWB, groups, units)
        sent, (r_late, natural) = after(sent, (r_late, natural))
        first.append(swap(sent, "pair"))
    first.append(r_late)
    sums = gram(r_late, arrive_0, order_0)

    v_sent = [
        pack(basis, send_v, straight(part, c * part), ROWB, groups, units) for c in range(2)
    ]
    v_sent[0], (first[0], sums, natural) = after(v_sent[0], (first[0], sums, natural))
    if early:
        sums = gram(first[0], arrive_0, order_0, sums)
    v_got = [swap(v_sent[0], "pair"), None]
    turns = turns_of(lax.psum(sums, "slab"))

    def second(sources, row0, size):
        turned = rotate(sources, arrive_0, order_0, turns, row0, size)
        return pack(turned, send_1, straight(size), ROWB, groups, units)

    late_chunks, row0 = [], 0
    for lo, hi in bounds[1 if early else 0 :]:
        size = (hi - lo) * slabs * ROWB
        late_chunks.append((first[-1], row0, size))
        row0 += size
    early_chunks = [(first[0], 0, early * slabs * ROWB)] if early else []
    r_two, last = [], v_got[0]
    for sources, row0, size in late_chunks + early_chunks:
        sent = second(sources, row0, size)
        sent, last = after(sent, last)
        if r_two:
            r_two[-1] = last
        else:
            v_got[0] = last
        last = swap(sent, "pair")
        r_two.append(last)

    packed = [slab_pack(r_two[c], slabs) for c in range(len(late_chunks))]
    v_sent[1], r_two[-1] = after(v_sent[1], r_two[-1])
    v_got[1] = swap(v_sent[1], "pair")
    r_home = [over_slab(blocks) for blocks in packed]
    sums = None
    for got in r_two:
        sums = gram(got, arrive_1, order_1, sums)
    v_got[0], sums = after(v_got[0], sums)
    sums = lax.psum(sums, "slab")

    v_next, v_got[1] = after(second(v_got[0], 0, part), v_got[1])
    v_two = [swap(v_next, "pair")]
    (v_next, sums), v_two[0] = after((second(v_got[1], 0, part), sums), v_two[0])
    v_two.append(swap(v_next, "pair"))
    turns_1 = turns_of(sums)

    v_out = rotate(v_two[0], arrive_1, order_1, turns_1, 0, part, None, basis.shape, 0)
    r_out = None
    if early:
        r_out = settle(
            r_two[-1], arrive_1, order_1, natural[0], turns_1, strips, r_slabs.shape
        )
    for c, blocks in enumerate(r_home):
        r_out = settle(
            [blocks.reshape(-1, blocks.shape[2])],
            arrive_1,
            order_1,
            natural[c + early],
            turns_1,
            strips,
            r_slabs.shape,
            r_out,
        )
    v_two[1], (r_out, v_out) = after(v_two[1], (r_out, v_out))
    v_out = rotate(v_two[1], arrive_1, order_1, turns_1, 0, part, v_out, basis.shape, 1)
    return r_out, v_out


def solution(mesh):
    placed = (P("slab", "pair"), P("slab", "pair"), P("slab"), P())
    return jax.shard_map(
        functools.partial(shards, mesh.shape["pair"], mesh.shape["slab"]),
        mesh=mesh,
        in_specs=placed,
        out_specs=(P("slab", "pair"), P("slab", "pair")),
        check_vma=False,
    )
```

```python
import functools

import jax
import jax.numpy as jnp
from jax import lax
from jax.experimental import pallas as pl
from jax.experimental.pallas import tpu as pltpu
from jax.sharding import PartitionSpec as P

BLK = 192
ROWB = 48
WIN = 256
EPSILON = 1e-06
HIGH = lax.Precision.HIGH
VMEM_LIMIT = 48 * 1024 * 1024
SMALL = pl.CostEstimate(flops=1, bytes_accessed=1, transcendentals=0)


def rotations(cross_gram, norms_a, norms_b):
    width = cross_gram.shape[-1]
    scale_a = lax.rsqrt(norms_a)
    scale_b = lax.rsqrt(norms_b)
    normed = cross_gram * scale_a[:, :, None] * scale_b[:, None, :]
    frobenius = jnp.sqrt(jnp.sum(normed * normed, axis=(1, 2)))
    coupling = normed / (1.0 + frobenius)[:, None, None]
    outer_a = jnp.einsum("pik,pjk->pij", coupling, coupling, precision=HIGH)
    outer_b = jnp.einsum("pki,pkj->pij", coupling, coupling, precision=HIGH)
    identity = jnp.eye(width, dtype=cross_gram.dtype)
    left_poly = (
        identity
        - 0.5 * outer_a
        + 0.375 * jnp.einsum("pik,pkj->pij", outer_a, outer_a, precision=HIGH)
    )
    right_poly = (
        identity
        - 0.5 * outer_b
        + 0.375 * jnp.einsum("pik,pkj->pij", outer_b, outer_b, precision=HIGH)
    )
    upper_half = jnp.concatenate(
        [left_poly, -jnp.einsum("pik,pkj->pij", coupling, right_poly, precision=HIGH)], axis=2
    )
    lower_half = jnp.concatenate(
        [jnp.einsum("pki,pkj->pij", coupling, left_poly, precision=HIGH), right_poly], axis=2
    )
    return jnp.concatenate([upper_half, lower_half], axis=1)


def turns_of(sums):
    cross_gram = sums[:, :BLK, :BLK]
    norms_a = sums[:, BLK, :BLK] + EPSILON
    norms_b = sums[:, BLK + 1, :BLK] + EPSILON
    return rotations(cross_gram, norms_a, norms_b)


def move_tables(place, me, groups, count):
    total = place.shape[0]
    units = count // groups
    slots = jnp.arange(total, dtype=jnp.int32)
    source, local = place // count, place % count
    target = slots // count
    same = (target[:, None] == target[None, :]) & (source[:, None] == source[None, :])
    rank = jnp.sum((same & (slots[None, :] < slots[:, None])).astype(jnp.int32), axis=1)
    offset = jnp.arange(groups, dtype=jnp.int32)
    unit = jnp.arange(units, dtype=jnp.int32)
    chosen = (
        (source == me)[None, None, :]
        & (target[None, None, :] == (me ^ offset)[:, None, None])
        & (rank[None, None, :] == unit[None, :, None])
    )
    send = jnp.sum(jnp.where(chosen, local[None, None, :], 0), axis=2).reshape(groups * units)
    mine = lax.dynamic_slice_in_dim(source ^ me, me * count, count)
    order = lax.dynamic_slice_in_dim(rank, me * count, count)
    return send, mine, order


def rank_among(kind):
    index = jnp.arange(kind.shape[-1], dtype=jnp.int32)
    same = (kind[..., :, None] == kind[..., None, :]) & (index[None, :] < index[:, None])
    return jnp.sum(same.astype(jnp.int32), axis=-1)


def shifted(window, left):
    return pltpu.roll(window, WIN - 64 if left else 64, 1)


def low_half(window, odd):
    return jnp.where(odd == 1, shifted(window, True), window)


def merge(first, first_odd, second, second_odd):
    a = low_half(first, first_odd)
    b = jnp.where(second_odd == 1, second, shifted(second, False))
    lane = lax.broadcasted_iota(jnp.int32, (first.shape[0], 128), 1)
    middle = jnp.where(lane < 64, a[:, 128:], b[:, :128])
    return jnp.concatenate([a[:, :128], middle, b[:, 128:]], axis=1)


def unit_width(units):
    return max(WIN, units * BLK)


def pack_kernel(groups, units, blocks, send, rows_at, *refs):
    sources, outs = refs[:blocks], refs[blocks:]
    size = sources[0].shape[0]
    for i, x_ref in enumerate(sources):
        rows = slice(i * size, (i + 1) * size)

        def window(place):
            block = send[place]
            strip = (3 * block) // 2
            return x_ref[:, pl.ds(pl.multiple_of(strip * 128, 128), WIN)], block % 2

        for group in range(groups):
            if units == 1:
                w, odd = window(group)
                outs[group][rows, :] = low_half(w, odd)
            for j in range(0, units - 1, 2):
                w0, odd0 = window(group * units + j)
                w1, odd1 = window(group * units + j + 1)
                outs[group][rows, BLK * j : BLK * (j + 2)] = merge(w0, odd0, w1, odd1)


def pack(x, send, rows_at, block_rows, groups, units):
    total = rows_at.shape[0]
    blocks = 4 if total % 4 == 0 else 1
    width = unit_width(units)

    def block_at(k):
        return pl.BlockSpec(
            (block_rows, x.shape[1]), lambda i, send, at: (at[i * blocks + k], 0)
        )

    return pl.pallas_call(
        functools.partial(pack_kernel, groups, units, blocks),
        grid_spec=pltpu.PrefetchScalarGridSpec(
            num_scalar_prefetch=2,
            grid=(total // blocks,),
            in_specs=[block_at(k) for k in range(blocks)],
            out_specs=[pl.BlockSpec((blocks * block_rows, width), lambda i, *_: (i, 0))]
            * groups,
        ),
        out_shape=[jax.ShapeDtypeStruct((total * block_rows, width), jnp.float32)] * groups,
        compiler_params=pltpu.CompilerParams(vmem_limit_bytes=VMEM_LIMIT),
        cost_estimate=SMALL,
        name="pack",
    )(send, rows_at, *[x] * blocks)


def halves(x):
    high = x.astype(jnp.bfloat16)
    return high, (x - high.astype(jnp.float32)).astype(jnp.bfloat16)


def product(a, b, dims):
    (ah, al), (bh, bl) = a, b
    dot = functools.partial(
        lax.dot_general, dimension_numbers=(dims, ((), ())), preferred_element_type=jnp.float32
    )
    return dot(ah, bh) + (dot(al, bh) + dot(ah, bl))


def fetcher(arrive, order, sources, win, sems, row0, rows):
    def start(q, slot):
        for side in range(2):
            at = arrive[2 * q + side]
            strip = (3 * order[2 * q + side]) // 2
            for k, source in enumerate(sources):

                @pl.when(at == k)
                def _():
                    pltpu.make_async_copy(
                        source.at[
                            pl.ds(row0, rows), pl.ds(pl.multiple_of(strip * 128, 128), WIN)
                        ],
                        win.at[slot, side],
                        sems.at[slot, side],
                    ).start()

    def wait(slot):
        for side in range(2):
            pltpu.make_async_copy(
                sources[0].at[pl.ds(row0, rows), pl.ds(0, WIN)],
                win.at[slot, side],
                sems.at[slot, side],
            ).wait()

    return start, wait


def pipelined(start, wait):
    q, last = pl.program_id(0), pl.num_programs(0)
    slot = lax.rem(q, 2)

    @pl.when(q == 0)
    def _():
        start(0, 0)

    @pl.when(q + 1 < last)
    def _():
        start(q + 1, 1 - slot)

    wait(slot)
    return q, slot


def tile_of(rows):
    return 384 if rows % 384 == 0 else rows


def pair_tile(win, slot, start, tile):
    rows = pl.ds(pl.multiple_of(start, 8), tile)
    return jnp.concatenate([win[slot, 0, rows, :], win[slot, 1, rows, :]], axis=1)


def spread(turn, odd, other_odd):
    gap = jnp.zeros((WIN - BLK, 2 * BLK), jnp.float32)

    def placed(part, odd):
        return jnp.where(
            odd == 1, jnp.concatenate([gap, part]), jnp.concatenate([part, gap])
        )

    return jnp.concatenate([placed(turn[:BLK], odd), placed(turn[BLK:], other_odd)])


def long_halves(turn):
    high, low = halves(turn)
    return jnp.concatenate([high, high, low])


def turned_tile(x, long_turn):
    high, low = halves(x)
    return jnp.dot(
        jnp.concatenate([high, low, high], axis=1), long_turn, preferred_element_type=jnp.float32
    )


def gram_kernel(groups, given, arrive, order, *refs):
    sources, earlier = refs[:groups], refs[groups : groups + given]
    out, win, sems = refs[groups + given :]
    rows = win.shape[2]
    q, slot = pipelined(*fetcher(arrive, order, sources, win, sems, 0, rows))
    tile = tile_of(rows)
    total = jnp.zeros((WIN, WIN), jnp.float32)
    squares = jnp.zeros((8, 2 * WIN), jnp.float32)
    for step in range(rows // tile):
        x = pair_tile(win, slot, step * tile, tile)
        high, low = halves(x)
        total += product(
            (high[:, :WIN], low[:, :WIN]), (high[:, WIN:], low[:, WIN:]), ((0,), (0,))
        )
        squares += jnp.sum((x * x).reshape(tile // 8, 8, 2 * WIN), axis=0)
    odd, other_odd = order[2 * q] % 2, order[2 * q + 1] % 2
    total = jnp.where(odd == 1, total[WIN - BLK :], total[:BLK])
    out[0, :BLK, :] = low_half(total, other_odd)
    norms = jnp.broadcast_to(jnp.sum(squares, axis=0, keepdims=True), (8, 2 * WIN))
    row = lax.broadcasted_iota(jnp.int32, (8, WIN), 0)
    out[0, BLK:, :] = jnp.where(
        row == 0, low_half(norms[:, :WIN], odd), low_half(norms[:, WIN:], other_odd)
    )
    for sums in earlier:
        out[...] += sums[...]


def gram(sources, arrive, order, earlier=None):
    groups, rows = len(sources), sources[0].shape[0]
    given = [] if earlier is None else [earlier]
    sums = pl.BlockSpec((1, BLK + 8, WIN), lambda q, *_: (q, 0, 0))
    pairs = arrive.shape[0] // 2
    return pl.pallas_call(
        functools.partial(gram_kernel, groups, len(given)),
        grid_spec=pltpu.PrefetchScalarGridSpec(
            num_scalar_prefetch=2,
            grid=(pairs,),
            in_specs=[pl.BlockSpec(memory_space=pl.ANY)] * groups + [sums] * len(given),
            out_specs=sums,
            scratch_shapes=[
                pltpu.VMEM((2, 2, rows, WIN), jnp.float32),
                pltpu.SemaphoreType.DMA((2, 2)),
            ],
        ),
        out_shape=jax.ShapeDtypeStruct((pairs, BLK + 8, WIN), jnp.float32),
        compiler_params=pltpu.CompilerParams(vmem_limit_bytes=VMEM_LIMIT),
        cost_estimate=SMALL,
        name="cross_products",
    )(arrive, order, *sources, *given)


def rotate_kernel(groups, row0, given, arrive, order, *refs):
    sources, turn = refs[:groups], refs[groups]
    out, win, sems = refs[groups + 1 + given :]
    rows = win.shape[2]
    q, slot = pipelined(*fetcher(arrive, order, sources, win, sems, row0, rows))
    tile = tile_of(rows)
    long_turn = long_halves(spread(turn[0], order[2 * q] % 2, order[2 * q + 1] % 2))
    for step in range(rows // tile):
        x = pair_tile(win, slot, step * tile, tile)
        out[step * tile : (step + 1) * tile, :] = turned_tile(x, long_turn)


def rotate(sources, arrive, order, turns, row0, rows, into=None, shape=None, at=0):
    groups = len(sources)
    pairs = arrive.shape[0] // 2
    shape = shape or (rows, pairs * 2 * BLK)
    given = [] if into is None else [into]
    return pl.pallas_call(
        functools.partial(rotate_kernel, groups, row0, len(given)),
        grid_spec=pltpu.PrefetchScalarGridSpec(
            num_scalar_prefetch=2,
            grid=(pairs,),
            in_specs=[pl.BlockSpec(memory_space=pl.ANY)] * groups
            + [pl.BlockSpec((1, 2 * BLK, 2 * BLK), lambda q, *_: (q, 0, 0))]
            + [pl.BlockSpec(memory_space=pl.ANY)] * len(given),
            out_specs=pl.BlockSpec((rows, 2 * BLK), lambda q, *_: (at, q)),
            scratch_shapes=[
                pltpu.VMEM((2, 2, rows, WIN), jnp.float32),
                pltpu.SemaphoreType.DMA((2, 2)),
            ],
        ),
        out_shape=jax.ShapeDtypeStruct(shape, jnp.float32),
        input_output_aliases={groups + 3: 0} if given else {},
        compiler_params=pltpu.CompilerParams(vmem_limit_bytes=VMEM_LIMIT),
        cost_estimate=SMALL,
        name="rotate",
    )(arrive, order, *sources, turns, *given)


def gather_kernel(rows_at, x_ref, out, held, in_sems, out_sems):
    count = out.shape[0]

    def arrival(i):
        start = pl.multiple_of(rows_at[i] * ROWB, 8)
        return pltpu.make_async_copy(
            x_ref.at[pl.ds(start, ROWB), :], held.at[i], in_sems.at[i]
        )

    def departure(i):
        return pltpu.make_async_copy(held.at[i], out.at[i], out_sems.at[i])

    for i in range(count):
        arrival(i).start()
    for i in range(count):
        arrival(i).wait()
        departure(i).start()
    for i in range(count):
        departure(i).wait()


def gather_rows(x, rows_at):
    count = rows_at.shape[0]
    shape = (count, ROWB, x.shape[1])
    return pl.pallas_call(
        gather_kernel,
        grid_spec=pltpu.PrefetchScalarGridSpec(
            num_scalar_prefetch=1,
            grid=(1,),
            in_specs=[pl.BlockSpec(memory_space=pl.ANY)],
            out_specs=pl.BlockSpec(memory_space=pl.ANY),
            scratch_shapes=[
                pltpu.VMEM(shape, jnp.float32),
                pltpu.SemaphoreType.DMA((count,)),
                pltpu.SemaphoreType.DMA((count,)),
            ],
        ),
        out_shape=jax.ShapeDtypeStruct(shape, jnp.float32),
        compiler_params=pltpu.CompilerParams(vmem_limit_bytes=VMEM_LIMIT),
        cost_estimate=SMALL,
        name="gather_rows",
    )(rows_at, x)


def slab_pack_kernel(groups, *refs):
    sources, (out, held, in_sems, out_sems) = refs[:groups], refs[groups:]
    slabs, rows, _ = out.shape
    width = sources[0].shape[1]
    arrivals = []
    for o in range(slabs):
        for g in range(groups):
            copy = pltpu.make_async_copy(
                sources[g].at[pl.ds(o * rows, rows), :],
                held.at[o, :, pl.ds(g * width, width)],
                in_sems.at[o, g],
            )
            copy.start()
            arrivals.append(copy)
    departures = []
    for o in range(slabs):
        for copy in arrivals[o * groups : (o + 1) * groups]:
            copy.wait()
        copy = pltpu.make_async_copy(held.at[o], out.at[o], out_sems.at[o])
        copy.start()
        departures.append(copy)
    for copy in departures:
        copy.wait()


def slab_pack(sources, slabs):
    groups = len(sources)
    rows, width = sources[0].shape[0] // slabs, sources[0].shape[1]
    shape = (slabs, rows, groups * width)
    return pl.pallas_call(
        functools.partial(slab_pack_kernel, groups),
        in_specs=[pl.BlockSpec(memory_space=pl.ANY)] * groups,
        out_specs=pl.BlockSpec(memory_space=pl.ANY),
        scratch_shapes=[
            pltpu.VMEM(shape, jnp.float32),
            pltpu.SemaphoreType.DMA((slabs, groups)),
            pltpu.SemaphoreType.DMA((slabs,)),
        ],
        out_shape=jax.ShapeDtypeStruct(shape, jnp.float32),
        compiler_params=pltpu.CompilerParams(vmem_limit_bytes=VMEM_LIMIT),
        cost_estimate=SMALL,
        name="slab_pack",
    )(*sources)


def settle_kernel(groups, strips, given, arrive, order, natural, *refs):
    sources, turn = refs[:groups], refs[groups]
    out, win, done, sems, out_sems = refs[groups + 1 + given :]
    rows = win.shape[2]
    if groups == 1:
        source = sources[0]

        def start(q, slot):
            for side in range(2):
                strip = arrive[2 * q + side] * strips + (3 * order[2 * q + side]) // 2
                pltpu.make_async_copy(
                    source.at[:, pl.ds(pl.multiple_of(strip * 128, 128), WIN)],
                    win.at[slot, side],
                    sems.at[slot, side],
                ).start()

        _, wait = fetcher(arrive, order, sources, win, sems, 0, rows)
    else:
        start, wait = fetcher(arrive, order, sources, win, sems, 0, rows)

    q, slot = pipelined(start, wait)
    tile = tile_of(rows)
    long_turn = long_halves(spread(turn[0], order[2 * q] % 2, order[2 * q + 1] % 2))

    def written(at):
        pltpu.make_async_copy(done.at[at], done.at[at], out_sems.at[at]).wait()

    @pl.when(q >= 2)
    def _():
        written(slot)

    for step in range(rows // tile):
        x = pair_tile(win, slot, step * tile, tile)
        done[slot, step * tile : (step + 1) * tile, :] = turned_tile(x, long_turn)

    columns = pl.ds(pl.multiple_of(q * 2 * BLK, 128), 2 * BLK)
    for block in range(rows // ROWB):
        pltpu.make_async_copy(
            done.at[slot, pl.ds(block * ROWB, ROWB), :],
            out.at[pl.ds(pl.multiple_of(natural[block] * ROWB, 8), ROWB), columns],
            out_sems.at[slot],
        ).start()

    @pl.when(q == pl.num_programs(0) - 1)
    def _():
        written(slot)

        @pl.when(q >= 1)
        def _():
            written(1 - slot)


def settle(sources, arrive, order, natural, turns, strips, shape, into=None):
    groups, rows = len(sources), sources[0].shape[0]
    pairs = arrive.shape[0] // 2
    given = [] if into is None else [into]
    return pl.pallas_call(
        functools.partial(settle_kernel, groups, strips, len(given)),
        grid_spec=pltpu.PrefetchScalarGridSpec(
            num_scalar_prefetch=3,
            grid=(pairs,),
            in_specs=[pl.BlockSpec(memory_space=pl.ANY)] * groups
            + [pl.BlockSpec((1, 2 * BLK, 2 * BLK), lambda q, *_: (q, 0, 0))]
            + [pl.BlockSpec(memory_space=pl.ANY)] * len(given),
            out_specs=pl.BlockSpec(memory_space=pl.ANY),
            scratch_shapes=[
                pltpu.VMEM((2, 2, rows, WIN), jnp.float32),
                pltpu.VMEM((2, rows, 2 * BLK), jnp.float32),
                pltpu.SemaphoreType.DMA((2, 2)),
                pltpu.SemaphoreType.DMA((2,)),
            ],
        ),
        out_shape=jax.ShapeDtypeStruct(shape, jnp.float32),
        input_output_aliases={groups + 4: 0} if given else {},
        compiler_params=pltpu.CompilerParams(vmem_limit_bytes=VMEM_LIMIT),
        cost_estimate=SMALL,
        name="settle",
    )(arrive, order, natural, *sources, turns, *given)


def swap(arrays, axis):
    count = len(arrays)
    return [arrays[0]] + [
        lax.ppermute(arrays[o], axis, [(i, i ^ o) for i in range(count)]) for o in range(1, count)
    ]


def after(arrays, earlier):
    return lax.optimization_barrier((arrays, earlier))


def shards(groups, slabs, r_slabs, basis, owners, plan):
    rows = r_slabs.shape[0]
    count = r_slabs.shape[1] // BLK
    units = count // groups
    strips = unit_width(units) // 128
    row_blocks = owners.shape[0]
    each = row_blocks // slabs
    early = 1 if each > 1 else 0
    late = each - early
    late_cuts = [1, late - 1] if late > 1 else [late]
    part = rows // 2
    pair_index = lax.axis_index("pair")
    slab_index = lax.axis_index("slab")

    send_0, arrive_0, order_0 = move_tables(plan[0], pair_index, groups, count)
    slot_ids = jnp.arange(plan.shape[1], dtype=jnp.int32)
    place_1 = jnp.sum(
        jnp.where(plan[0][None, :] == plan[1][:, None], slot_ids[None, :], 0), axis=1
    )
    send_1, arrive_1, order_1 = move_tables(place_1, pair_index, groups, count)

    goes_to = owners // row_blocks
    rank = rank_among(goes_to)
    bounds, low = [], 0
    for size in [early] * (early > 0) + late_cuts:
        bounds.append((low, low + size))
        low += size
    spot = sum(
        jnp.where(
            (rank >= lo) & (rank < hi), slabs * lo + goes_to * (hi - lo) + rank - lo, 0
        )
        for lo, hi in bounds
    )
    index = jnp.arange(row_blocks, dtype=jnp.int32)
    rows_at = jnp.sum(jnp.where(spot[None, :] == index[:, None], index[None, :], 0), axis=1)
    table = lax.all_gather(owners, "slab", axis=0, tiled=True).reshape(slabs, row_blocks)
    table_to = table // row_blocks
    table_rank = rank_among(table_to)
    per_rank = jnp.arange(each, dtype=jnp.int32)
    hit = (table_to == slab_index)[:, None, :] & (table_rank[:, None, :] == per_rank[None, :, None])
    where_to = jnp.sum(jnp.where(hit, (table % row_blocks)[:, None, :], 0), axis=2)
    natural = [where_to[:, lo:hi].reshape(slabs * (hi - lo)) for lo, hi in bounds]

    def straight(size, start=0):
        return jnp.arange(size // ROWB, dtype=jnp.int32) + start // ROWB

    def over_slab(blocks):
        return lax.all_to_all(blocks, "slab", 0, 0, tiled=True)

    r_late, last, send, rows_early = [], None, send_0, rows_at[: slabs * early]
    for lo, hi in bounds[1 if early else 0 :]:
        sent = pack(r_slabs, send, rows_at[slabs * lo : slabs * hi], ROWB, groups, units)
        if last is None:
            send, sent = after(send, sent)
        else:
            rows_early, last[1] = after(rows_early, last[1])
            gathered = gather_rows(r_slabs, rows_early)
            (sent, gathered), r_late[-1] = after((sent, gathered), last)
        last = swap(sent, "pair")
        r_late.append(last)
    first = []
    if early:
        home = over_slab(gathered).reshape(-1, r_slabs.shape[1])
        sent = pack(home, send_0, straight(home.shape[0]), ROWB, groups, units)
        sent, (r_late[-1], natural) = after(sent, (r_late[-1], natural))
        first.append(swap(sent, "pair"))
    first += r_late
    sums = None
    for got in r_late:
        sums = gram(got, arrive_0, order_0, sums)

    v_sent = [
        pack(basis, send, straight(part, c * part), ROWB, groups, units) for c in range(2)
    ]
    v_sent[0], (first[0], sums, natural) = after(v_sent[0], (first[0], sums, natural))
    if early:
        sums = gram(first[0], arrive_0, order_0, sums)
    v_got = [swap(v_sent[0], "pair"), None]
    turns = turns_of(lax.psum(sums, "slab"))

    def second(sources, row0, size):
        turned = rotate(sources, arrive_0, order_0, turns, row0, size)
        return pack(turned, send_1, straight(size), ROWB, groups, units)

    r_two, last = [], v_got[0]
    for sources in first[early:] + first[:early]:
        sent = second(sources, 0, sources[0].shape[0])
        sent, last = after(sent, last)
        if r_two:
            r_two[-1] = last
        else:
            v_got[0] = last
        last = swap(sent, "pair")
        r_two.append(last)

    packed = [slab_pack(r_two[c], slabs) for c in range(len(r_late))]
    v_sent[1], r_two[-1] = after(v_sent[1], r_two[-1])
    v_got[1] = swap(v_sent[1], "pair")
    r_home = [over_slab(blocks) for blocks in packed]
    sums = None
    for got in r_two:
        sums = gram(got, arrive_1, order_1, sums)
    v_got[0], sums = after(v_got[0], sums)
    sums = lax.psum(sums, "slab")

    v_next, v_got[1] = after(second(v_got[0], 0, part), v_got[1])
    v_two = [swap(v_next, "pair")]
    (v_next, sums), v_two[0] = after((second(v_got[1], 0, part), sums), v_two[0])
    v_two.append(swap(v_next, "pair"))
    turns_1 = turns_of(sums)

    v_out = rotate(v_two[0], arrive_1, order_1, turns_1, 0, part, None, basis.shape, 0)
    r_out = None
    if early:
        r_out = settle(
            r_two[-1], arrive_1, order_1, natural[0], turns_1, strips, r_slabs.shape
        )
    for c, blocks in enumerate(r_home):
        r_out = settle(
            [blocks.reshape(-1, blocks.shape[2])],
            arrive_1,
            order_1,
            natural[c + early],
            turns_1,
            strips,
            r_slabs.shape,
            r_out,
        )
    v_two[1], (r_out, v_out) = after(v_two[1], (r_out, v_out))
    v_out = rotate(v_two[1], arrive_1, order_1, turns_1, 0, part, v_out, basis.shape, 1)
    return r_out, v_out


def solution(mesh):
    placed = (P("slab", "pair"), P("slab", "pair"), P("slab"), P())
    return jax.shard_map(
        functools.partial(shards, mesh.shape["pair"], mesh.shape["slab"]),
        mesh=mesh,
        in_specs=placed,
        out_specs=(P("slab", "pair"), P("slab", "pair")),
        check_vma=False,
    )
```
